512 devices in a mesh: facet: 16 (over z), col: 32 (over x, y, core).
Axes of the slice: x: 4, y: 4, z: 16, core: 2. Of those that a mesh axis runs over, the one named last changes fastest.
Arguments:
- sky_re: bfloat16 [16, 4096, 4096], P('facet', None, 'col'), may hold values from -6 to 6
- sky_im: bfloat16 [16, 4096, 4096], P('facet', None, 'col'), may hold values from -6 to 6
- col_offsets: int32 [2], replicated, may hold values from 0 to 65280
- sub_offsets: int32 [16], replicated, may hold values from 0 to 65280
- kernel: float32 [16, 8], replicated, may hold values from 0.05 to 1
- vis_count: int32 [16, 128], P('facet', 'col'), may hold values from 0 to 128, as said below
- cell_index: int32 [2, 16, 128, 128], P(None, 'facet', 'col'), may hold values from 0 to 248
- frac_index: int32 [2, 16, 128, 128], P(None, 'facet', 'col'), may hold values from 0 to 15
Outputs:
- vis_re: float32 [16, 128, 128], P('facet', 'col')
- vis_im: float32 [16, 128, 128], P('facet', 'col')
The draws below stay inside these ranges and needn't reach their ends.
Inputs may be any that keep to these rules, and one draw needn't show every extreme that they name: Within each subgrid the blocks with visibilities come first and block 0 holds 128; in some subgrid all 128 blocks hold visibilities; a block's visibilities fill its first vis_count slots.
All inputs are finite; a program needn't handle non-finite values.
Results may differ from the reference program's by a relative error of at most 0.0037.
Values may be sent and summed in bfloat16 or wider, within the bound.
No kernel may reach another device: no remote copies, remote signals or barrier semaphores. Data moves between devices by JAX's collectives and lax.ppermute only.
A program may use at most 64 MiB of HBM per device.

```python
import math
import jax
import jax.numpy as jnp
from jax import lax

N_IMG = 65536
M = 4096
S = 256
KS = 8
OS = 16
SCOL = 2
VB = 128
NSUB = 16
BLK_SUB = 128
N_FACET = 16


def draw_vis_count(key, part):
    key_full, key_live, key_counts = jax.random.split(jax.random.fold_in(key, 11), 3)
    full_index = jax.random.randint(key_full, (), 0, NSUB)
    raw_draws = jax.random.randint(key_live, (NSUB,), 1, BLK_SUB + 1)
    live_blocks = jnp.maximum(1, raw_draws * raw_draws // BLK_SUB)
    live_blocks = jnp.where(jnp.arange(NSUB) == full_index, BLK_SUB, live_blocks)
    counts = jax.random.randint(key_counts, (NSUB, BLK_SUB), 1, VB + 1)
    block_ids = jnp.arange(BLK_SUB)[None, :]
    counts = jnp.where(block_ids == 0, VB, counts)
    return jnp.where(block_ids < live_blocks[:, None], counts, 0).astype(jnp.int32)


def place_ends(drawn, own_key, smallest, top_value):
    shape = drawn.shape
    index_at = [jax.random.randint(jax.random.fold_in(own_key, axis), (), 0, shape[axis]) for axis in range(len(shape))]
    drawn = drawn.at[tuple(index_at)].set(smallest)
    longest = shape.index(max(shape))
    index_at[longest] = (index_at[longest] + 1) % shape[longest]
    return drawn.at[tuple(index_at)].set(top_value)


def level_of(rng, extent, shards, smallest, high):
    def one(axis_at, shards_of):
        draws = jax.random.uniform(jax.random.fold_in(jax.random.fold_in(rng, 6), axis_at), (shards_of,), jnp.float32, smallest / len(shards), high / len(shards))
        return jnp.repeat(jnp.exp(draws), extent[axis_at] // shards_of).reshape((-1,) + (1,) * (len(extent) - axis_at - 1))

    level = one(*shards[0])
    for cut in shards[1:]:
        level = level * one(*cut)
    return level


def centred(stream_key, shape, scale, bound, cuts=(), kind=jnp.bfloat16):
    array = jax.random.normal(stream_key, shape, jnp.float32) * scale
    if len(cuts) > 0:
        array = level_of(stream_key, shape, cuts, -0.22, 0.18) * array
    return jnp.clip(array, min=-bound, max=bound).astype(kind)


def setup_inputs(seed: int = 0) -> dict:
    arg_keys = jax.random.split(jax.random.key(seed), 9)
    sky_re = centred(arg_keys[0], (N_FACET, M, M), 1.0, 6.0, ((0, 16), (2, 32)))
    sky_im = centred(arg_keys[1], (N_FACET, M, M), 1.0, 6.0, ((0, 16), (2, 32)))
    col_offsets = jax.random.randint(arg_keys[2], (SCOL,), 0, N_IMG - S + 1).astype(jnp.int32)
    sub_offsets = place_ends(jax.random.randint(arg_keys[3], (NSUB,), 0, N_IMG - S + 1), jax.random.fold_in(arg_keys[3], 1), 0, N_IMG - S).astype(jnp.int32)
    kernel = jnp.clip(jnp.exp(jax.random.uniform(arg_keys[4], (OS, KS), jnp.float32, math.log(0.05), math.log(1.0))), 0.05, 1.0)
    vis_count = draw_vis_count(jax.random.fold_in(arg_keys[8], 71), 0)
    cell_index = place_ends(jax.random.randint(arg_keys[6], (2, NSUB, BLK_SUB, VB), 0, S - KS + 1), jax.random.fold_in(arg_keys[6], 1), 0, S - KS).astype(jnp.int32)
    frac_index = place_ends(jax.random.randint(arg_keys[7], (2, NSUB, BLK_SUB, VB), 0, OS), jax.random.fold_in(arg_keys[7], 1), 0, OS - 1).astype(jnp.int32)
    return {"sky_re": sky_re, "sky_im": sky_im, "col_offsets": col_offsets, "sub_offsets": sub_offsets, "kernel": kernel, "vis_count": vis_count, "cell_index": cell_index, "frac_index": frac_index}


def modular_product(left_ints, right_ints):
    upper_part = right_ints // 256
    lower_part = right_ints % 256
    product = left_ints[:, None] * upper_part[None, :] % N_IMG
    product = product * 256 % N_IMG
    return (product + left_ints[:, None] * lower_part[None, :]) % N_IMG

def cos_sin(left_ints, right_ints, factor):
    angles = modular_product(left_ints, right_ints).astype(jnp.float32) * (2.0 * math.pi / N_IMG)
    return (jnp.cos(angles) * factor, jnp.sin(angles) * factor)

def first_axis(facet_image, table, local_cols):
    product = jnp.dot(table, facet_image, preferred_element_type=jnp.float32)
    real_part = product[:S, :local_cols] + product[S:, local_cols:]
    imag_part = product[:S, local_cols:] - product[S:, :local_cols]
    return jnp.stack([real_part, imag_part]).astype(jnp.bfloat16)

def second_axis(band_rows, starts, anchor, second_table):
    mod_cos, mod_sin = cos_sin(starts, anchor, 1.0)
    shifted_re = band_rows[0][None] * mod_cos[:, None] + band_rows[1][None] * mod_sin[:, None]
    shifted_im = band_rows[1][None] * mod_cos[:, None] - band_rows[0][None] * mod_sin[:, None]
    stacked = jnp.concatenate([shifted_re, shifted_im], axis=0).astype(jnp.bfloat16)
    per_column = starts.shape[0]
    row_count = band_rows.shape[1]
    product = jnp.dot(stacked.reshape(2 * per_column * row_count, -1), second_table, preferred_element_type=jnp.float32)
    product = product.reshape(2, per_column, row_count, 2 * S)
    term_re = product[0, :, :, :S] + product[1, :, :, S:]
    term_im = product[1, :, :, :S] - product[0, :, :, S:]
    return jnp.concatenate([term_re, term_im], axis=2)

def lookup(frac_ints, kernel):
    table_rows = jnp.arange(kernel.shape[0], dtype=jnp.int32)
    matches = frac_ints[..., None] == table_rows
    return lax.optimization_barrier(jnp.sum(jnp.where(matches[..., None], kernel, 0.0), axis=-2))

def reference(sky_re, sky_im, col_offsets, sub_offsets, kernel, vis_count, cell_index, frac_index):
    spatial = jnp.arange(M, dtype=jnp.int32)
    spectral = jnp.arange(S, dtype=jnp.int32)
    per_column = NSUB // SCOL
    first_tables = []
    for column in range(SCOL):
        cos_part, sin_part = cos_sin(col_offsets[column] + spectral, spatial, 1.0 / math.sqrt(M))
        first_tables.append(jnp.concatenate([cos_part, sin_part], axis=0).astype(jnp.bfloat16))

    def facet_step(running, inputs):
        real_part, imag_part, facet_index = inputs
        facet_image = jnp.concatenate([real_part, imag_part], axis=1)
        anchor = facet_index * M + spatial
        cos_tab, sin_tab = cos_sin(anchor, spectral, 1.0 / math.sqrt(M * N_FACET))
        second_table = jnp.concatenate([cos_tab, sin_tab], axis=1).astype(jnp.bfloat16)
        column_terms = []
        for column in range(SCOL):
            band_rows = first_axis(facet_image, first_tables[column], M)
            starts = sub_offsets[column * per_column:(column + 1) * per_column]
            column_terms.append(second_axis(band_rows, starts, anchor, second_table))
        return (running + jnp.concatenate(column_terms, axis=0), None)
    initial = jnp.zeros((NSUB, S, 2 * S), jnp.float32)
    subgrids, _ = lax.scan(facet_step, initial, (sky_re, sky_im, jnp.arange(N_FACET, dtype=jnp.int32)))
    subgrids = subgrids.astype(jnp.bfloat16)
    offsets = jnp.arange(KS, dtype=jnp.int32)
    slot_ids = jnp.arange(VB, dtype=jnp.int32)

    def one_subgrid(inputs):
        subgrid, cell_rows, frac_rows, counts = inputs

        def one_block(block_inputs):
            cell_block, frac_block, slot_count = block_inputs
            row_taps = lookup(frac_block[0], kernel).astype(jnp.bfloat16)
            row_taps = lax.optimization_barrier(row_taps).astype(jnp.float32)
            col_taps = lookup(frac_block[1], kernel)
            gathered = jnp.take(subgrid, cell_block[0][:, None] + offsets, axis=0).astype(jnp.float32)
            row_sum = jnp.einsum('va,vac->vc', row_taps, gathered, precision=lax.Precision.HIGHEST)
            col_ids = cell_block[1][:, None] + offsets
            picked_re = jnp.take_along_axis(row_sum[:, :S], col_ids, axis=1)
            picked_im = jnp.take_along_axis(row_sum[:, S:], col_ids, axis=1)
            in_block = slot_ids < slot_count
            vis_real = jnp.where(in_block, lax.optimization_barrier(jnp.sum(picked_re * col_taps, axis=1)), 0.0)
            vis_imag = jnp.where(in_block, lax.optimization_barrier(jnp.sum(picked_im * col_taps, axis=1)), 0.0)
            return (vis_real, vis_imag)
        return lax.map(one_block, (jnp.moveaxis(cell_rows, 1, 0), jnp.moveaxis(frac_rows, 1, 0), counts))
    vis_real, vis_imag = lax.map(one_subgrid, (subgrids, jnp.moveaxis(cell_index, 1, 0), jnp.moveaxis(frac_index, 1, 0), vis_count))
    return (vis_real, vis_imag)
```

```python
import math

import jax
import jax.numpy as jnp
from jax import lax
from jax.experimental import pallas as pl
from jax.experimental.pallas import tpu as pltpu
from jax.sharding import PartitionSpec as P

N_IMG = 65536
S = 256
SCOL = 2
LANES = 128
CHUNK = 512
PARAMS = pltpu.CompilerParams(vmem_limit_bytes=48 * 1024 * 1024)
VMEM = pl.BlockSpec(memory_space=pltpu.VMEM)
SMEM = pl.BlockSpec(memory_space=pltpu.SMEM)
f32 = jnp.float32
bf16 = jnp.bfloat16


def cos_sin(p):
    q = (p + 8192) >> 14
    x = (p - (q << 14)).astype(f32) * (2.0 * math.pi / N_IMG)
    x2 = x * x
    s = x * (1.0 + x2 * (-1.0 / 6 + x2 * (1.0 / 120 + x2 * (-1.0 / 5040 + x2 * (1.0 / 362880)))))
    c = 1.0 + x2 * (-0.5 + x2 * (1.0 / 24 + x2 * (-1.0 / 720 + x2 * (1.0 / 40320))))
    odd = (q & 1) == 1
    a = jnp.where(odd, s, c)
    b = jnp.where(odd, c, s)
    return jnp.where(((q + 1) & 2) == 2, -a, a), jnp.where((q & 2) == 2, -b, b)


def cmul(ac, as_, bc, bs):
    return ac * bc - as_ * bs, as_ * bc + ac * bs


def first_axis_kernel(col_ref, re_ref, im_ref, out_ref, high_ref, table_ref, acc_ref):
    step = pl.program_id(0)
    pixels = lax.broadcasted_iota(jnp.int32, (16, CHUNK), 1) + step * CHUNK
    row = lax.broadcasted_iota(jnp.int32, (16, CHUNK), 0)
    high_c, high_s = cos_sin(row * 16 * pixels)
    high_ref[0] = high_c
    high_ref[1] = high_s
    low_c, low_s = cos_sin(row * pixels)
    for q in range(SCOL):
        off_c, off_s = cos_sin(pixels[:8] * col_ref[q])
        off_c = jnp.concatenate([off_c, off_c], axis=0) * (1.0 / 64)
        off_s = jnp.concatenate([off_s, off_s], axis=0) * (1.0 / 64)
        base_c, base_s = cmul(low_c, low_s, off_c, off_s)
        for h in range(16):
            tc, ts = cmul(base_c, base_s, high_ref[0, h : h + 1, :], high_ref[1, h : h + 1, :])
            table_ref[q * 512 + h * 16 : q * 512 + h * 16 + 16, :] = tc.astype(bf16)
            table_ref[q * 512 + 256 + h * 16 : q * 512 + 256 + h * 16 + 16, :] = ts.astype(bf16)
    image = jnp.concatenate([re_ref[...], im_ref[...]], axis=1)
    product = jnp.dot(table_ref[...], image, preferred_element_type=f32)

    @pl.when(step == 0)
    def _():
        acc_ref[...] = product

    @pl.when(step > 0)
    def _():
        acc_ref[...] += product

    @pl.when(step == pl.num_programs(0) - 1)
    def _():
        for q in range(SCOL):
            cos_part = acc_ref[q * 512 : q * 512 + 256, :]
            sin_part = acc_ref[q * 512 + 256 : q * 512 + 512, :]
            real = (cos_part[:, :LANES] + sin_part[:, LANES:]).reshape(32, 8, LANES)
            imag = (cos_part[:, LANES:] - sin_part[:, :LANES]).reshape(32, 8, LANES)
            out_ref[:, q * 16 : q * 16 + 16, :] = jnp.concatenate([real, imag], axis=1).astype(bf16)


def first_axis(col_offsets, sky_re, sky_im):
    pixels = sky_re.shape[0]
    block = pl.BlockSpec((CHUNK, LANES), lambda i: (i, 0))
    return pl.pallas_call(
        first_axis_kernel,
        grid=(pixels // CHUNK,),
        in_specs=[SMEM, block, block],
        out_specs=pl.BlockSpec((32, 32, LANES), lambda i: (0, 0, 0)),
        out_shape=jax.ShapeDtypeStruct((32, 32, LANES), bf16),
        scratch_shapes=[
            pltpu.VMEM((2, 16, CHUNK), f32),
            pltpu.VMEM((1024, CHUNK), bf16),
            pltpu.VMEM((1024, 256), f32),
        ],
        compiler_params=PARAMS,
        name="first_axis",
    )(col_offsets, sky_re, sky_im)


def second_table_kernel(start_ref, sub_ref, table_ref, shift_ref, high_ref):
    start = start_ref[0]
    cells = lax.broadcasted_iota(jnp.int32, (16, S), 1)
    row = lax.broadcasted_iota(jnp.int32, (16, S), 0)
    low_c, low_s = cos_sin(row * cells)
    low_c = low_c * (1.0 / 256)
    low_s = low_s * (1.0 / 256)
    all_cells = lax.broadcasted_iota(jnp.int32, (256, S), 1)
    all_rows = lax.broadcasted_iota(jnp.int32, (256, S), 0)
    high_c, high_s = cos_sin((start + 16 * all_rows) * all_cells)
    high_ref[0] = high_c
    high_ref[1] = high_s

    def body(i, carry):
        for u in range(8):
            h = i * 8 + u
            tc, ts = cmul(low_c, low_s, high_ref[0, pl.ds(h, 1), :], high_ref[1, pl.ds(h, 1), :])
            table_ref[pl.ds(pl.multiple_of(h * 16, 16), 16), :] = jnp.concatenate([tc, ts], axis=1).astype(bf16)
        return carry

    lax.fori_loop(0, 32, body, 0)
    n_sub = shift_ref.shape[0] // 2
    offs = sub_ref[...]
    for at in range(0, shift_ref.shape[1], 1024):
        y = lax.broadcasted_iota(jnp.int32, (n_sub, 1024), 1) + (start + at)
        c, d = cos_sin(offs * y)
        shift_ref[:n_sub, at : at + 1024] = c
        shift_ref[n_sub:, at : at + 1024] = d


def second_tables(start, sub_offsets, pixels):
    n_sub = sub_offsets.shape[0]
    return pl.pallas_call(
        second_table_kernel,
        in_specs=[SMEM, VMEM],
        out_specs=[VMEM, VMEM],
        out_shape=[
            jax.ShapeDtypeStruct((pixels, 2 * S), bf16),
            jax.ShapeDtypeStruct((2 * n_sub, pixels), f32),
        ],
        scratch_shapes=[pltpu.VMEM((2, 256, S), f32)],
        compiler_params=PARAMS,
        name="second_tables",
    )(start, sub_offsets.reshape(n_sub, 1))


def second_axis_kernel(band_ref, shift_ref, table_ref, out_ref, lhs_ref, acc_ref):
    step = pl.program_id(0)
    n_sub = shift_ref.shape[0] // 2
    for c in range(band_ref.shape[0]):
        lanes = slice(c * LANES, (c + 1) * LANES)
        for q in range(SCOL):
            band = band_ref[c, q * 16 : q * 16 + 16, :].astype(f32)
            re, im = band[:8], band[8:]
            for s in range(q * n_sub // SCOL, (q + 1) * n_sub // SCOL):
                mc = shift_ref[s : s + 1, lanes]
                md = shift_ref[n_sub + s : n_sub + s + 1, lanes]
                both = jnp.concatenate([re * mc + im * md, im * mc - re * md], axis=0)
                lhs_ref[s * 16 : s * 16 + 16, lanes] = both.astype(bf16)
    product = jnp.dot(lhs_ref[...], table_ref[...], preferred_element_type=f32)

    @pl.when(step == 0)
    def _():
        acc_ref[...] = product

    @pl.when(step > 0)
    def _():
        acc_ref[...] += product

    @pl.when(step == pl.num_programs(0) - 1)
    def _():
        total = acc_ref[...].reshape(n_sub, 16, 2 * S)
        re = total[:, :8, :S] + total[:, 8:, S:]
        im = total[:, 8:, :S] - total[:, :8, S:]
        out_ref[:, :S] = re.reshape(n_sub * 8, S).astype(bf16)
        out_ref[:, S:] = im.reshape(n_sub * 8, S).astype(bf16)


def second_axis(band, shift, table):
    pixels = table.shape[0]
    n_sub = shift.shape[0] // 2
    wide = 1024
    return pl.pallas_call(
        second_axis_kernel,
        grid=(pixels // wide,),
        in_specs=[
            pl.BlockSpec((wide // LANES, 32, LANES), lambda i: (i, 0, 0)),
            pl.BlockSpec((2 * n_sub, wide), lambda i: (0, i)),
            pl.BlockSpec((wide, 2 * S), lambda i: (i, 0)),
        ],
        out_specs=pl.BlockSpec((n_sub * 8, 2 * S), lambda i: (0, 0)),
        out_shape=jax.ShapeDtypeStruct((n_sub * 8, 2 * S), bf16),
        scratch_shapes=[
            pltpu.VMEM((n_sub * 16, wide), bf16),
            pltpu.VMEM((n_sub * 16, 2 * S), f32),
        ],
        compiler_params=PARAMS,
        name="second_axis",
    )(band, shift, table)


def own_rows_kernel(terms_ref, out_ref):
    total = terms_ref[0].astype(f32)
    for f in range(1, terms_ref.shape[0]):
        total = total + terms_ref[f].astype(f32)
    rows = total.astype(bf16)
    for c in range(out_ref.shape[0]):
        out_ref[c] = rows


def own_rows(terms, copies):
    return pl.pallas_call(
        own_rows_kernel,
        in_specs=[VMEM],
        out_specs=VMEM,
        out_shape=jax.ShapeDtypeStruct((copies, *terms.shape[1:]), bf16),
        compiler_params=PARAMS,
        name="own_rows",
    )(terms)


def weights_kernel(kernel_ref, cell_ref, frac_ref, row_ref, high_ref, low_ref):
    blocks, slots = cell_ref.shape[1:]
    for b in range(blocks):
        lanes = slice(b * slots, (b + 1) * slots)
        for axis in range(2):
            frac = frac_ref[axis, b : b + 1, :]
            ahead = lax.broadcasted_iota(jnp.int32, (S, slots), 0) - cell_ref[axis, b : b + 1, :]
            spread = jnp.zeros((S, slots), f32)
            for a in range(kernel_ref.shape[1]):
                tap = jnp.zeros((1, slots), f32)
                for o in range(kernel_ref.shape[0]):
                    tap = jnp.where(frac == o, kernel_ref[o, a], tap)
                spread = jnp.where(ahead == a, tap, spread)
            if axis == 0:
                row_ref[:, lanes] = spread.astype(bf16)
            else:
                high = spread.astype(bf16)
                high_ref[:, lanes] = high
                low_ref[:, lanes] = (spread - high.astype(f32)).astype(bf16)


def weights(kernel, cells, fracs):
    total = cells.shape[1] * cells.shape[2]
    shape = jax.ShapeDtypeStruct((S, total), bf16)
    return pl.pallas_call(
        weights_kernel,
        in_specs=[SMEM, VMEM, VMEM],
        out_specs=[VMEM] * 3,
        out_shape=[shape] * 3,
        compiler_params=PARAMS,
        name="weights",
    )(kernel, cells, fracs)


def degrid_kernel(count_ref, grid_ref, row_ref, high_ref, low_ref, re_ref, im_ref):
    blocks, slots = re_ref.shape
    row = row_ref[...].astype(f32)
    for part, out_ref in ((0, re_ref), (1, im_ref)):
        cells = grid_ref[:, part * S : (part + 1) * S]
        sums = jnp.dot(cells, high_ref[...], preferred_element_type=f32)
        sums = sums + jnp.dot(cells, low_ref[...], preferred_element_type=f32)
        values = jnp.sum(sums * row, axis=0, keepdims=True)
        for b in range(blocks):
            live = lax.broadcasted_iota(jnp.int32, (1, slots), 1) < count_ref[b]
            out_ref[b : b + 1, :] = jnp.where(live, values[:, b * slots : (b + 1) * slots], 0.0)


def degrid(counts, grid, row, high, low, blocks, slots):
    shape = jax.ShapeDtypeStruct((blocks, slots), f32)
    return pl.pallas_call(
        degrid_kernel,
        in_specs=[SMEM] + [VMEM] * 4,
        out_specs=[VMEM] * 2,
        out_shape=[shape] * 2,
        compiler_params=PARAMS,
        name="degrid",
    )(counts, grid, row, high, low)


def exchange(x, axis):
    return lax.all_to_all(x, axis, split_axis=0, concat_axis=0, tiled=True)


def local(sky_re, sky_im, col_offsets, sub_offsets, kernel, vis_count, cell_index, frac_index):
    pixels = sky_re.shape[1]
    n_sub = sub_offsets.shape[0]
    col = lax.axis_size("col")
    blocks, slots = cell_index.shape[2:]
    band = exchange(first_axis(col_offsets, sky_re[0], sky_im[0]), "col")
    start = (lax.axis_index("facet") * pixels).astype(jnp.int32).reshape(1)
    table, shift = second_tables(start, sub_offsets, pixels)
    terms = second_axis(band, shift, table)
    arrived = exchange(terms.reshape(n_sub, 8, 2 * S), "facet")
    row, high, low = weights(kernel, cell_index[:, 0], frac_index[:, 0])
    grid = exchange(own_rows(arrived, col), "col").reshape(S, 2 * S)
    vis_re, vis_im = degrid(vis_count[0], grid, row, high, low, blocks, slots)
    return vis_re[None], vis_im[None]


def solution(mesh):
    placed = (
        P("facet", None, "col"),
        P("facet", None, "col"),
        P(),
        P(),
        P(),
        P("facet", "col"),
        P(None, "facet", "col", None),
        P(None, "facet", "col", None),
    )
    return jax.shard_map(
        local,
        mesh=mesh,
        in_specs=placed,
        out_specs=(P("facet", "col", None), P("facet", "col", None)),
        check_vma=False,
    )
```

```python
import math

import jax
import jax.numpy as jnp
from jax import lax
from jax.experimental import pallas as pl
from jax.experimental.pallas import tpu as pltpu
from jax.sharding import PartitionSpec as P

N_IMG = 65536
S = 256
SCOL = 2
LANES = 128
PAIRS = 4
LOADS = 4
READY = 3072
PARAMS = pltpu.CompilerParams(vmem_limit_bytes=16 * 1024 * 1024)
MIDDLE = pltpu.CompilerParams(vmem_limit_bytes=24 * 1024 * 1024)
WIDE = pltpu.CompilerParams(vmem_limit_bytes=60 * 1024 * 1024)
VMEM = pl.BlockSpec(memory_space=pltpu.VMEM)
SMEM = pl.BlockSpec(memory_space=pltpu.SMEM)
HBM = pl.BlockSpec(memory_space=pltpu.HBM)
f32 = jnp.float32
bf16 = jnp.bfloat16


def cos_sin(p):
    q = (p + 8192) >> 14
    x = (p - (q << 14)).astype(f32) * (2.0 * math.pi / N_IMG)
    x2 = x * x
    s = x * (1.0 + x2 * (-1.0 / 6 + x2 * (1.0 / 120 + x2 * (-1.0 / 5040 + x2 * (1.0 / 362880)))))
    c = 1.0 + x2 * (-0.5 + x2 * (1.0 / 24 + x2 * (-1.0 / 720 + x2 * (1.0 / 40320))))
    odd = (q & 1) == 1
    a = jnp.where(odd, s, c)
    b = jnp.where(odd, c, s)
    return jnp.where(((q + 1) & 2) == 2, -a, a), jnp.where((q & 2) == 2, -b, b)


def cmul(ac, as_, bc, bs):
    return ac * bc - as_ * bs, as_ * bc + ac * bs


def row_phases(mult, scale, blocks):
    lane = lax.broadcasted_iota(jnp.int32, (8, LANES), 1)
    low_c, low_s = cos_sin(mult * lane)
    high_c, high_s = cos_sin(mult * (lane * LANES))
    low_c, low_s = low_c * scale, low_s * scale
    return [cmul(low_c, low_s, high_c[:, b : b + 1], high_s[:, b : b + 1]) for b in range(blocks)]


def first_axis_kernel(col_hbm, re_hbm, im_hbm, out_ref, col_ref, sky_ref, base_ref, step_ref, sem):
    pixels = re_hbm.shape[0]
    blocks = pixels // LANES
    part = pixels // LOADS
    col_copy = pltpu.make_async_copy(col_hbm, col_ref, sem.at[0])
    col_copy.start()
    copies = []
    for i in range(LOADS):
        for k, src in enumerate((re_hbm, im_hbm)):
            rows = pl.ds(i * part, part)
            dst = sky_ref.at[rows, pl.ds(k * LANES, LANES)]
            copies.append(pltpu.make_async_copy(src.at[rows], dst, sem.at[1 + 2 * i + k]))
            copies[-1].start()
    row = lax.broadcasted_iota(jnp.int32, (8, LANES), 0)
    near = row_phases(row * 8, 1.0, blocks)
    far = row_phases(row * 64, 1.0, blocks)
    for b in range(blocks):
        lanes = slice(b * LANES, (b + 1) * LANES)
        (near_c, near_s), (far_c, far_s) = near[b], far[b]
        next_c, next_s = cmul(near_c, near_s, far_c[1:2], far_s[1:2])
        for k, rows in enumerate(((near_c, next_c, far_c), (near_s, next_s, far_s))):
            for i in range(3):
                step_ref[k, 8 * i : 8 * i + 8, lanes] = rows[i]
    col_copy.wait()
    for q in range(SCOL):
        middle = row_phases(row + (col_ref[q] + 128), 1.0 / 64, blocks)
        for b in range(blocks):
            lanes = slice(b * LANES, (b + 1) * LANES)
            base_ref[q, 0, :, lanes] = middle[b][0]
            base_ref[q, 1, :, lanes] = middle[b][1]

    def table_rows(q, first):
        cols = []
        for b in range(blocks):
            lanes = slice(b * LANES, (b + 1) * LANES)
            bc, bs = base_ref[q, 0, :, lanes], base_ref[q, 1, :, lanes]
            up_c, up_s, down_c, down_s = [], [], [], []
            for d in range(first, first + PAIRS):
                at = 18 if d == 16 else d
                hc, hs = step_ref[0, at : at + 1, lanes], step_ref[1, at : at + 1, lanes]
                cc, ss, sc, cs = bc * hc, bs * hs, bs * hc, bc * hs
                up_c.append(bc if d == 16 else cc - ss)
                up_s.append(bs if d == 16 else sc + cs)
                down_c.append(cc + ss)
                down_s.append(sc - cs)
            cols.append(jnp.concatenate(up_c + up_s + down_c + down_s, axis=0).astype(bf16))
        return jnp.concatenate(cols, axis=1)

    for copy in copies:
        copy.wait()
    for q in range(SCOL):
        for first in range(1, 17, PAIRS):
            product = jnp.dot(table_rows(q, first), sky_ref[...], preferred_element_type=f32)
            side = 8 * PAIRS
            for k in range(2):
                c = product[2 * k * side : (2 * k + 1) * side]
                s = product[(2 * k + 1) * side : (2 * k + 2) * side]
                real = c[:, :LANES] + s[:, LANES:]
                imag = c[:, LANES:] - s[:, :LANES]
                for t in range(PAIRS):
                    d = first + t
                    group = 16 - d if k == 1 else 16 if d == 16 else 16 + d
                    rows = slice(8 * t, 8 * t + 8)
                    both = jnp.concatenate([real[rows], imag[rows]], axis=0)
                    out_ref[group, q * 16 : q * 16 + 16, :] = both.astype(bf16)


def first_axis(col_offsets, sky_re, sky_im):
    pixels = sky_re.shape[0]
    return pl.pallas_call(
        first_axis_kernel,
        in_specs=[HBM] * 3,
        out_specs=VMEM,
        out_shape=jax.ShapeDtypeStruct((32, 32, LANES), bf16),
        scratch_shapes=[
            pltpu.SMEM((SCOL,), jnp.int32),
            pltpu.VMEM((pixels, 2 * LANES), bf16),
            pltpu.VMEM((SCOL, 2, 8, pixels), f32),
            pltpu.VMEM((2, 24, pixels), f32),
            pltpu.SemaphoreType.DMA((1 + 2 * LOADS,)),
        ],
        compiler_params=WIDE,
        name="first_axis",
    )(col_offsets, sky_re, sky_im)


def table_blocks(start, step_ref, blocks):
    cells = lax.broadcasted_iota(jnp.int32, (8, S), 1)
    row = lax.broadcasted_iota(jnp.int32, (8, S), 0)
    for i in range(2):
        c, s = cos_sin((row + 8 * i) * 8 * cells)
        step_ref[0, 8 * i : 8 * i + 8, :] = c
        step_ref[1, 8 * i : 8 * i + 8, :] = s
    last = cos_sin(cells[:1] * 128)
    base_c, base_s = cos_sin((row + 128) * cells)
    base_c, base_s = base_c * (1.0 / 256), base_s * (1.0 / 256)
    block = lax.broadcasted_iota(jnp.int32, (16, S), 0)
    block_c, block_s = cos_sin((start + 256 * block) * lax.broadcasted_iota(jnp.int32, (16, S), 1))
    made = []
    for g in blocks:
        bc, bs = cmul(base_c, base_s, block_c[g : g + 1], block_s[g : g + 1])
        up, down = [], []
        for d in range(1, 17):
            hc, hs = last if d == 16 else (step_ref[0, d : d + 1, :], step_ref[1, d : d + 1, :])
            cc, ss, sc, cs = bc * hc, bs * hs, bs * hc, bc * hs
            if d < 16:
                up.append(jnp.concatenate([cc - ss, sc + cs], axis=1))
            down.append(jnp.concatenate([cc + ss, sc - cs], axis=1))
        rows = down[::-1] + [jnp.concatenate([bc, bs], axis=1)] + up
        made.append(jnp.concatenate(rows, axis=0).astype(bf16))
    return made


def second_table_kernel(start_ref, table_ref, step_ref):
    blocks = range(table_ref.shape[0] // 256)
    for g, made in zip(blocks, table_blocks(start_ref[0], step_ref, blocks)):
        table_ref[g * 256 : (g + 1) * 256, :] = made


def second_table(start, rows):
    return pl.pallas_call(
        second_table_kernel,
        in_specs=[SMEM],
        out_specs=VMEM,
        out_shape=jax.ShapeDtypeStruct((rows, 2 * S), bf16),
        scratch_shapes=[pltpu.VMEM((2, 16, S), f32)],
        compiler_params=PARAMS,
        name="second_table",
    )(start)


def second_axis_kernel(start_ref, sub_ref, band_ref, ready_ref, out_ref, shift_ref, table_ref, step_ref):
    n_sub = sub_ref.shape[0]
    chunks = band_ref.shape[0]
    per = n_sub // SCOL
    start = start_ref[0]
    ready = ready_ref.shape[0]
    row = lax.broadcasted_iota(jnp.int32, (n_sub, LANES), 0)
    lane = lax.broadcasted_iota(jnp.int32, (n_sub, LANES), 1)
    offs = jnp.zeros((n_sub, LANES), jnp.int32)
    for s in range(n_sub):
        offs = jnp.where(row == s, sub_ref[s], offs)
    low_c, low_s = cos_sin(offs * lane)
    high_c, high_s = cos_sin(offs * (lane * LANES + start))
    for b in range(chunks):
        lanes = slice(b * LANES, (b + 1) * LANES)
        c, d = cmul(low_c, low_s, high_c[:, b : b + 1], high_s[:, b : b + 1])
        shift_ref[0, :, lanes] = c
        shift_ref[1, :, lanes] = d
    for g, made in enumerate(table_blocks(start, step_ref, range(ready // 256, chunks // 2))):
        table_ref[g * 256 : (g + 1) * 256, :] = made

    def shifted(q):
        cols = []
        for c in range(chunks):
            lanes = slice(c * LANES, (c + 1) * LANES)
            band = band_ref[c, q * 16 : q * 16 + 16, :].astype(f32)
            re, im = band[:8], band[8:]
            rows = []
            for s in range(q * per, (q + 1) * per):
                mc = shift_ref[0, s : s + 1, lanes]
                md = shift_ref[1, s : s + 1, lanes]
                rows += [re * mc + im * md, im * mc - re * md]
            cols.append(jnp.concatenate(rows, axis=0).astype(bf16))
        return jnp.concatenate(cols, axis=1)

    left = jnp.concatenate([shifted(q) for q in range(SCOL)], axis=0)
    product = jnp.dot(left[:, :ready], ready_ref[...], preferred_element_type=f32)
    product = product + jnp.dot(left[:, ready:], table_ref[...], preferred_element_type=f32)
    product = product.reshape(n_sub, 16, 2 * S)
    re = product[:, :8, :S] + product[:, 8:, S:]
    im = product[:, 8:, :S] - product[:, :8, S:]
    out_ref[:, :S] = re.reshape(n_sub * 8, S).astype(bf16)
    out_ref[:, S:] = im.reshape(n_sub * 8, S).astype(bf16)


def second_axis(start, sub_offsets, band, ready):
    n_sub = sub_offsets.shape[0]
    pixels = band.shape[0] * LANES
    return pl.pallas_call(
        second_axis_kernel,
        in_specs=[SMEM, SMEM, VMEM, VMEM],
        out_specs=VMEM,
        out_shape=jax.ShapeDtypeStruct((n_sub * 8, 2 * S), bf16),
        scratch_shapes=[
            pltpu.VMEM((2, n_sub, pixels), f32),
            pltpu.VMEM((pixels - ready.shape[0], 2 * S), bf16),
            pltpu.VMEM((2, 16, S), f32),
        ],
        compiler_params=MIDDLE,
        name="second_axis",
    )(start, sub_offsets, band, ready)


def own_rows_kernel(terms_ref, out_ref):
    total = terms_ref[0].astype(f32)
    for f in range(1, terms_ref.shape[0]):
        total = total + terms_ref[f].astype(f32)
    rows = total.astype(bf16)
    for c in range(out_ref.shape[0]):
        out_ref[c] = rows


def own_rows(terms, copies):
    return pl.pallas_call(
        own_rows_kernel,
        in_specs=[VMEM],
        out_specs=VMEM,
        out_shape=jax.ShapeDtypeStruct((copies, *terms.shape[1:]), bf16),
        compiler_params=PARAMS,
        name="own_rows",
    )(terms)


def weights_kernel(kernel_ref, cell_ref, frac_ref, row_ref, high_ref, low_ref):
    blocks, slots = cell_ref.shape[1:]
    for b in range(blocks):
        lanes = slice(b * slots, (b + 1) * slots)
        for axis in range(2):
            frac = frac_ref[axis, b : b + 1, :]
            ahead = lax.broadcasted_iota(jnp.int32, (S, slots), 0) - cell_ref[axis, b : b + 1, :]
            spread = jnp.zeros((S, slots), f32)
            for a in range(kernel_ref.shape[1]):
                tap = jnp.zeros((1, slots), f32)
                for o in range(kernel_ref.shape[0]):
                    tap = jnp.where(frac == o, kernel_ref[o, a], tap)
                spread = jnp.where(ahead == a, tap, spread)
            if axis == 0:
                row_ref[:, lanes] = spread.astype(bf16)
            else:
                high = spread.astype(bf16)
                high_ref[:, lanes] = high
                low_ref[:, lanes] = (spread - high.astype(f32)).astype(bf16)


def weights(kernel, cells, fracs):
    total = cells.shape[1] * cells.shape[2]
    shape = jax.ShapeDtypeStruct((S, total), bf16)
    return pl.pallas_call(
        weights_kernel,
        in_specs=[SMEM, VMEM, VMEM],
        out_specs=[VMEM] * 3,
        out_shape=[shape] * 3,
        compiler_params=PARAMS,
        name="weights",
    )(kernel, cells, fracs)


def degrid_kernel(count_ref, grid_ref, row_ref, high_ref, low_ref, re_ref, im_ref):
    blocks, slots = re_ref.shape
    row = row_ref[...].astype(f32)
    for part, out_ref in ((0, re_ref), (1, im_ref)):
        cells = grid_ref[:, part * S : (part + 1) * S]
        sums = jnp.dot(cells, high_ref[...], preferred_element_type=f32)
        sums = sums + jnp.dot(cells, low_ref[...], preferred_element_type=f32)
        values = jnp.sum(sums * row, axis=0, keepdims=True)
        for b in range(blocks):
            live = lax.broadcasted_iota(jnp.int32, (1, slots), 1) < count_ref[b]
            out_ref[b : b + 1, :] = jnp.where(live, values[:, b * slots : (b + 1) * slots], 0.0)


def degrid(counts, grid, row, high, low, blocks, slots):
    shape = jax.ShapeDtypeStruct((blocks, slots), f32)
    return pl.pallas_call(
        degrid_kernel,
        in_specs=[SMEM] + [VMEM] * 4,
        out_specs=[VMEM] * 2,
        out_shape=[shape] * 2,
        compiler_params=PARAMS,
        name="degrid",
    )(counts, grid, row, high, low)


def exchange(x, axis):
    return lax.all_to_all(x, axis, split_axis=0, concat_axis=0, tiled=True)


def local(sky_re, sky_im, col_offsets, sub_offsets, kernel, vis_count, cell_index, frac_index):
    pixels = sky_re.shape[1]
    n_sub = sub_offsets.shape[0]
    col = lax.axis_size("col")
    blocks, slots = cell_index.shape[2:]
    band = exchange(first_axis(col_offsets, sky_re[0], sky_im[0]), "col")
    start = (lax.axis_index("facet") * pixels).astype(jnp.int32).reshape(1)
    terms = second_axis(start, sub_offsets, band, second_table(start, READY))
    arrived = exchange(terms.reshape(n_sub, 8, 2 * S), "facet")
    row, high, low = weights(kernel, cell_index[:, 0], frac_index[:, 0])
    grid = exchange(own_rows(arrived, col), "col").reshape(S, 2 * S)
    vis_re, vis_im = degrid(vis_count[0], grid, row, high, low, blocks, slots)
    return vis_re[None], vis_im[None]


def solution(mesh):
    placed = (
        P("facet", None, "col"),
        P("facet", None, "col"),
        P(),
        P(),
        P(),
        P("facet", "col"),
        P(None, "facet", "col", None),
        P(None, "facet", "col", None),
    )
    return jax.shard_map(
        local,
        mesh=mesh,
        in_specs=placed,
        out_specs=(P("facet", "col", None), P("facet", "col", None)),
        check_vma=False,
    )
```

```python
import math

import jax
import jax.numpy as jnp
from jax import lax
from jax.experimental import pallas as pl
from jax.experimental.pallas import tpu as pltpu
from jax.sharding import PartitionSpec as P

N_IMG = 65536
S = 256
SCOL = 2
LANES = 128
PAIRS = 4
LOADS = 4
READY = 2304
PARAMS = pltpu.CompilerParams(vmem_limit_bytes=16 * 1024 * 1024)
MIDDLE = pltpu.CompilerParams(vmem_limit_bytes=24 * 1024 * 1024)
WIDE = pltpu.CompilerParams(vmem_limit_bytes=60 * 1024 * 1024)
VMEM = pl.BlockSpec(memory_space=pltpu.VMEM)
SMEM = pl.BlockSpec(memory_space=pltpu.SMEM)
HBM = pl.BlockSpec(memory_space=pltpu.HBM)
f32 = jnp.float32
bf16 = jnp.bfloat16


def cos_sin(p):
    q = (p + 8192) >> 14
    x = (p - (q << 14)).astype(f32) * (2.0 * math.pi / N_IMG)
    x2 = x * x
    s = x * (1.0 + x2 * (-1.0 / 6 + x2 * (1.0 / 120 + x2 * (-1.0 / 5040 + x2 * (1.0 / 362880)))))
    c = 1.0 + x2 * (-0.5 + x2 * (1.0 / 24 + x2 * (-1.0 / 720 + x2 * (1.0 / 40320))))
    odd = (q & 1) == 1
    a = jnp.where(odd, s, c)
    b = jnp.where(odd, c, s)
    return jnp.where(((q + 1) & 2) == 2, -a, a), jnp.where((q & 2) == 2, -b, b)


def cmul(ac, as_, bc, bs):
    return ac * bc - as_ * bs, as_ * bc + ac * bs


def row_phases(mult, scale, blocks):
    lane = lax.broadcasted_iota(jnp.int32, (8, LANES), 1)
    low_c, low_s = cos_sin(mult * lane)
    high_c, high_s = cos_sin(mult * (lane * LANES))
    low_c, low_s = low_c * scale, low_s * scale
    return [cmul(low_c, low_s, high_c[:, b : b + 1], high_s[:, b : b + 1]) for b in range(blocks)]


def first_axis_kernel(col_hbm, re_hbm, im_hbm, out_ref, col_ref, sky_ref, base_ref, step_ref, sem):
    pixels = re_hbm.shape[0]
    blocks = pixels // LANES
    part = pixels // LOADS
    col_copy = pltpu.make_async_copy(col_hbm, col_ref, sem.at[0])
    col_copy.start()
    copies = []
    for i in range(LOADS):
        for k, src in enumerate((re_hbm, im_hbm)):
            rows = pl.ds(i * part, part)
            dst = sky_ref.at[rows, pl.ds(k * LANES, LANES)]
            copies.append(pltpu.make_async_copy(src.at[rows], dst, sem.at[1 + 2 * i + k]))
            copies[-1].start()
    row = lax.broadcasted_iota(jnp.int32, (8, LANES), 0)
    near = row_phases(row * 8, 1.0, blocks)
    far = row_phases(row * 64, 1.0, blocks)
    for b in range(blocks):
        lanes = slice(b * LANES, (b + 1) * LANES)
        (near_c, near_s), (far_c, far_s) = near[b], far[b]
        next_c, next_s = cmul(near_c, near_s, far_c[1:2], far_s[1:2])
        for k, rows in enumerate(((near_c, next_c, far_c), (near_s, next_s, far_s))):
            for i in range(3):
                step_ref[k, 8 * i : 8 * i + 8, lanes] = rows[i]
    col_copy.wait()
    for q in range(SCOL):
        middle = row_phases(row + (col_ref[q] + 128), 1.0 / 64, blocks)
        for b in range(blocks):
            lanes = slice(b * LANES, (b + 1) * LANES)
            base_ref[q, 0, :, lanes] = middle[b][0]
            base_ref[q, 1, :, lanes] = middle[b][1]

    def table_rows(q, first):
        cols = []
        for b in range(blocks):
            lanes = slice(b * LANES, (b + 1) * LANES)
            bc, bs = base_ref[q, 0, :, lanes], base_ref[q, 1, :, lanes]
            up_c, up_s, down_c, down_s = [], [], [], []
            for d in range(first, first + PAIRS):
                at = 18 if d == 16 else d
                hc, hs = step_ref[0, at : at + 1, lanes], step_ref[1, at : at + 1, lanes]
                cc, ss, sc, cs = bc * hc, bs * hs, bs * hc, bc * hs
                up_c.append(bc if d == 16 else cc - ss)
                up_s.append(bs if d == 16 else sc + cs)
                down_c.append(cc + ss)
                down_s.append(sc - cs)
            cols.append(jnp.concatenate(up_c + up_s + down_c + down_s, axis=0).astype(bf16))
        return jnp.concatenate(cols, axis=1)

    for copy in copies:
        copy.wait()
    for q in range(SCOL):
        for first in range(1, 17, PAIRS):
            product = jnp.dot(table_rows(q, first), sky_ref[...], preferred_element_type=f32)
            side = 8 * PAIRS
            for k in range(2):
                c = product[2 * k * side : (2 * k + 1) * side]
                s = product[(2 * k + 1) * side : (2 * k + 2) * side]
                real = c[:, :LANES] + s[:, LANES:]
                imag = c[:, LANES:] - s[:, :LANES]
                for t in range(PAIRS):
                    d = first + t
                    group = 16 - d if k == 1 else 16 if d == 16 else 16 + d
                    rows = slice(8 * t, 8 * t + 8)
                    both = jnp.concatenate([real[rows], imag[rows]], axis=0)
                    out_ref[group, q * 16 : q * 16 + 16, :] = both.astype(bf16)


def first_axis(col_offsets, sky_re, sky_im):
    pixels = sky_re.shape[0]
    return pl.pallas_call(
        first_axis_kernel,
        in_specs=[HBM] * 3,
        out_specs=VMEM,
        out_shape=jax.ShapeDtypeStruct((32, 32, LANES), bf16),
        scratch_shapes=[
            pltpu.SMEM((SCOL,), jnp.int32),
            pltpu.VMEM((pixels, 2 * LANES), bf16),
            pltpu.VMEM((SCOL, 2, 8, pixels), f32),
            pltpu.VMEM((2, 24, pixels), f32),
            pltpu.SemaphoreType.DMA((1 + 2 * LOADS,)),
        ],
        compiler_params=WIDE,
        name="first_axis",
    )(col_offsets, sky_re, sky_im)


def table_blocks(start, step_ref, blocks):
    cells = lax.broadcasted_iota(jnp.int32, (8, S), 1)
    row = lax.broadcasted_iota(jnp.int32, (8, S), 0)
    for i in range(2):
        c, s = cos_sin((row + 8 * i) * 8 * cells)
        step_ref[0, 8 * i : 8 * i + 8, :] = c
        step_ref[1, 8 * i : 8 * i + 8, :] = s
    last = cos_sin(cells[:1] * 128)
    base_c, base_s = cos_sin((row + 128) * cells)
    base_c, base_s = base_c * (1.0 / 256), base_s * (1.0 / 256)
    block = lax.broadcasted_iota(jnp.int32, (16, S), 0)
    block_c, block_s = cos_sin((start + 256 * block) * lax.broadcasted_iota(jnp.int32, (16, S), 1))
    made = []
    for g in blocks:
        bc, bs = cmul(base_c, base_s, block_c[g : g + 1], block_s[g : g + 1])
        up, down = [], []
        for d in range(1, 17):
            hc, hs = last if d == 16 else (step_ref[0, d : d + 1, :], step_ref[1, d : d + 1, :])
            cc, ss, sc, cs = bc * hc, bs * hs, bs * hc, bc * hs
            if d < 16:
                up.append(jnp.concatenate([cc - ss, sc + cs], axis=1))
            down.append(jnp.concatenate([cc + ss, sc - cs], axis=1))
        rows = down[::-1] + [jnp.concatenate([bc, bs], axis=1)] + up
        made.append(jnp.concatenate(rows, axis=0).astype(bf16))
    return made


def second_table_kernel(start_ref, table_ref, step_ref):
    blocks = range(table_ref.shape[0] // 256)
    for g, made in zip(blocks, table_blocks(start_ref[0], step_ref, blocks)):
        table_ref[g * 256 : (g + 1) * 256, :] = made


def second_table(start, rows):
    return pl.pallas_call(
        second_table_kernel,
        in_specs=[SMEM],
        out_specs=VMEM,
        out_shape=jax.ShapeDtypeStruct((rows, 2 * S), bf16),
        scratch_shapes=[pltpu.VMEM((2, 16, S), f32)],
        compiler_params=PARAMS,
        name="second_table",
    )(start)


def second_axis_kernel(start_ref, sub_ref, band_ref, ready_ref, out_ref, shift_ref, table_ref, step_ref):
    n_sub = sub_ref.shape[0]
    chunks = band_ref.shape[0]
    per = n_sub // SCOL
    start = start_ref[0]
    ready = ready_ref.shape[0]
    row = lax.broadcasted_iota(jnp.int32, (n_sub, LANES), 0)
    lane = lax.broadcasted_iota(jnp.int32, (n_sub, LANES), 1)
    offs = jnp.zeros((n_sub, LANES), jnp.int32)
    for s in range(n_sub):
        offs = jnp.where(row == s, sub_ref[s], offs)
    low_c, low_s = cos_sin(offs * lane)
    high_c, high_s = cos_sin(offs * (lane * LANES + start))
    for b in range(chunks):
        lanes = slice(b * LANES, (b + 1) * LANES)
        c, d = cmul(low_c, low_s, high_c[:, b : b + 1], high_s[:, b : b + 1])
        shift_ref[0, :, lanes] = c
        shift_ref[1, :, lanes] = d
    for g, made in enumerate(table_blocks(start, step_ref, range(ready // 256, chunks // 2))):
        table_ref[g * 256 : (g + 1) * 256, :] = made

    def shifted(q):
        cols = []
        for c in range(chunks):
            lanes = slice(c * LANES, (c + 1) * LANES)
            band = band_ref[c, q * 16 : q * 16 + 16, :].astype(f32)
            re, im = band[:8], band[8:]
            rows = []
            for s in range(q * per, (q + 1) * per):
                mc = shift_ref[0, s : s + 1, lanes]
                md = shift_ref[1, s : s + 1, lanes]
                rows += [re * mc + im * md, im * mc - re * md]
            cols.append(jnp.concatenate(rows, axis=0).astype(bf16))
        return jnp.concatenate(cols, axis=1)

    left = jnp.concatenate([shifted(q) for q in range(SCOL)], axis=0)
    product = jnp.dot(left[:, :ready], ready_ref[...], preferred_element_type=f32)
    product = product + jnp.dot(left[:, ready:], table_ref[...], preferred_element_type=f32)
    product = product.reshape(n_sub, 16, 2 * S)
    re = product[:, :8, :S] + product[:, 8:, S:]
    im = product[:, 8:, :S] - product[:, :8, S:]
    out_ref[:, :S] = re.reshape(n_sub * 8, S).astype(bf16)
    out_ref[:, S:] = im.reshape(n_sub * 8, S).astype(bf16)


def second_axis(start, sub_offsets, band, ready):
    n_sub = sub_offsets.shape[0]
    pixels = band.shape[0] * LANES
    return pl.pallas_call(
        second_axis_kernel,
        in_specs=[SMEM, SMEM, VMEM, VMEM],
        out_specs=VMEM,
        out_shape=jax.ShapeDtypeStruct((n_sub * 8, 2 * S), bf16),
        scratch_shapes=[
            pltpu.VMEM((2, n_sub, pixels), f32),
            pltpu.VMEM((pixels - ready.shape[0], 2 * S), bf16),
            pltpu.VMEM((2, 16, S), f32),
        ],
        compiler_params=MIDDLE,
        name="second_axis",
    )(start, sub_offsets, band, ready)


def own_rows_kernel(terms_ref, out_ref):
    total = terms_ref[0].astype(f32)
    for f in range(1, terms_ref.shape[0]):
        total = total + terms_ref[f].astype(f32)
    rows = total.astype(bf16)
    for c in range(out_ref.shape[0]):
        out_ref[c] = rows


def own_rows(terms, copies):
    return pl.pallas_call(
        own_rows_kernel,
        in_specs=[VMEM],
        out_specs=VMEM,
        out_shape=jax.ShapeDtypeStruct((copies, *terms.shape[1:]), bf16),
        compiler_params=PARAMS,
        name="own_rows",
    )(terms)


def weights_kernel(kernel_ref, cell_ref, frac_ref, row_ref, col_ref):
    blocks, slots = cell_ref.shape[1:]
    for b in range(blocks):
        lanes = slice(b * slots, (b + 1) * slots)
        for axis in range(2):
            frac = frac_ref[axis, b : b + 1, :]
            ahead = lax.broadcasted_iota(jnp.int32, (S, slots), 0) - cell_ref[axis, b : b + 1, :]
            spread = jnp.zeros((S, slots), f32)
            for a in range(kernel_ref.shape[1]):
                tap = jnp.zeros((1, slots), f32)
                for o in range(kernel_ref.shape[0]):
                    tap = jnp.where(frac == o, kernel_ref[o, a], tap)
                spread = jnp.where(ahead == a, tap, spread)
            if axis == 0:
                row_ref[:, lanes] = spread.astype(bf16)
            else:
                high = spread.astype(bf16)
                col_ref[:S, lanes] = high
                col_ref[S:, lanes] = (spread - high.astype(f32)).astype(bf16)


def weights(kernel, cells, fracs):
    total = cells.shape[1] * cells.shape[2]
    return pl.pallas_call(
        weights_kernel,
        in_specs=[SMEM, VMEM, VMEM],
        out_specs=[VMEM] * 2,
        out_shape=[jax.ShapeDtypeStruct((S, total), bf16), jax.ShapeDtypeStruct((2 * S, total), bf16)],
        compiler_params=PARAMS,
        name="weights",
    )(kernel, cells, fracs)


def degrid_kernel(count_ref, grid_ref, row_ref, col_ref, re_ref, im_ref):
    blocks, slots = re_ref.shape
    row = row_ref[...].astype(f32)
    cells = jnp.concatenate([grid_ref[:, :S], grid_ref[:, S:]], axis=0)
    sums = jnp.dot(jnp.concatenate([cells, cells], axis=1), col_ref[...], preferred_element_type=f32)
    for part, out_ref in ((0, re_ref), (1, im_ref)):
        values = jnp.sum(sums[part * S : (part + 1) * S] * row, axis=0, keepdims=True)
        for b in range(blocks):
            live = lax.broadcasted_iota(jnp.int32, (1, slots), 1) < count_ref[b]
            out_ref[b : b + 1, :] = jnp.where(live, values[:, b * slots : (b + 1) * slots], 0.0)


def degrid(counts, grid, row, col, blocks, slots):
    shape = jax.ShapeDtypeStruct((blocks, slots), f32)
    return pl.pallas_call(
        degrid_kernel,
        in_specs=[SMEM] + [VMEM] * 3,
        out_specs=[VMEM] * 2,
        out_shape=[shape] * 2,
        compiler_params=PARAMS,
        name="degrid",
    )(counts, grid, row, col)


def exchange(x, axis):
    return lax.all_to_all(x, axis, split_axis=0, concat_axis=0, tiled=True)


def local(sky_re, sky_im, col_offsets, sub_offsets, kernel, vis_count, cell_index, frac_index):
    pixels = sky_re.shape[1]
    n_sub = sub_offsets.shape[0]
    col = lax.axis_size("col")
    blocks, slots = cell_index.shape[2:]
    band = exchange(first_axis(col_offsets, sky_re[0], sky_im[0]), "col")
    start = (lax.axis_index("facet") * pixels).astype(jnp.int32).reshape(1)
    row, column = weights(kernel, cell_index[:, 0], frac_index[:, 0])
    band, row, column = lax.optimization_barrier((band, row, column))
    terms = second_axis(start, sub_offsets, band, second_table(start, READY))
    arrived = exchange(terms.reshape(n_sub, 8, 2 * S), "facet")
    grid = exchange(own_rows(arrived, col), "col").reshape(S, 2 * S)
    vis_re, vis_im = degrid(vis_count[0], grid, row, column, blocks, slots)
    return vis_re[None], vis_im[None]


def solution(mesh):
    placed = (
        P("facet", None, "col"),
        P("facet", None, "col"),
        P(),
        P(),
        P(),
        P("facet", "col"),
        P(None, "facet", "col", None),
        P(None, "facet", "col", None),
    )
    return jax.shard_map(
        local,
        mesh=mesh,
        in_specs=placed,
        out_specs=(P("facet", "col", None), P("facet", "col", None)),
        check_vma=False,
    )
```

```python
import math

import jax
import jax.numpy as jnp
from jax import lax
from jax.experimental import pallas as pl
from jax.experimental.pallas import tpu as pltpu
from jax.sharding import PartitionSpec as P

N_IMG = 65536
S = 256
SCOL = 2
LANES = 128
PAIRS = 4
LOADS = 4
READY = 2304
PARAMS = pltpu.CompilerParams(vmem_limit_bytes=16 * 1024 * 1024)
MIDDLE = pltpu.CompilerParams(vmem_limit_bytes=24 * 1024 * 1024)
WIDE = pltpu.CompilerParams(vmem_limit_bytes=60 * 1024 * 1024)
VMEM = pl.BlockSpec(memory_space=pltpu.VMEM)
SMEM = pl.BlockSpec(memory_space=pltpu.SMEM)
HBM = pl.BlockSpec(memory_space=pltpu.HBM)
f32 = jnp.float32
bf16 = jnp.bfloat16


def cos_sin(p):
    q = (p + 8192) >> 14
    x = (p - (q << 14)).astype(f32) * (2.0 * math.pi / N_IMG)
    x2 = x * x
    s = x * (1.0 + x2 * (-1.0 / 6 + x2 * (1.0 / 120 + x2 * (-1.0 / 5040 + x2 * (1.0 / 362880)))))
    c = 1.0 + x2 * (-0.5 + x2 * (1.0 / 24 + x2 * (-1.0 / 720 + x2 * (1.0 / 40320))))
    odd = (q & 1) == 1
    a = jnp.where(odd, s, c)
    b = jnp.where(odd, c, s)
    return jnp.where(((q + 1) & 2) == 2, -a, a), jnp.where((q & 2) == 2, -b, b)


def cmul(ac, as_, bc, bs):
    return ac * bc - as_ * bs, as_ * bc + ac * bs


def row_phases(mult, scale, blocks):
    lane = lax.broadcasted_iota(jnp.int32, (8, LANES), 1)
    low_c, low_s = cos_sin(mult * lane)
    high_c, high_s = cos_sin(mult * (lane * LANES))
    low_c, low_s = low_c * scale, low_s * scale
    return [cmul(low_c, low_s, high_c[:, b : b + 1], high_s[:, b : b + 1]) for b in range(blocks)]


def first_axis_kernel(col_hbm, re_hbm, im_hbm, out_ref, col_ref, sky_ref, base_ref, step_ref, sem):
    pixels = re_hbm.shape[0]
    blocks = pixels // LANES
    part = pixels // LOADS
    col_copy = pltpu.make_async_copy(col_hbm, col_ref, sem.at[0])
    col_copy.start()
    copies = []
    for i in range(LOADS):
        for k, src in enumerate((re_hbm, im_hbm)):
            rows = pl.ds(i * part, part)
            dst = sky_ref.at[rows, pl.ds(k * LANES, LANES)]
            copies.append(pltpu.make_async_copy(src.at[rows], dst, sem.at[1 + 2 * i + k]))
            copies[-1].start()
    row = lax.broadcasted_iota(jnp.int32, (8, LANES), 0)
    near = row_phases(row * 8, 1.0, blocks)
    far = row_phases(row * 64, 1.0, blocks)
    for b in range(blocks):
        lanes = slice(b * LANES, (b + 1) * LANES)
        (near_c, near_s), (far_c, far_s) = near[b], far[b]
        next_c, next_s = cmul(near_c, near_s, far_c[1:2], far_s[1:2])
        for k, rows in enumerate(((near_c, next_c, far_c), (near_s, next_s, far_s))):
            for i in range(3):
                step_ref[k, 8 * i : 8 * i + 8, lanes] = rows[i]
    col_copy.wait()
    for q in range(SCOL):
        middle = row_phases(row + (col_ref[q] + 128), 1.0 / 64, blocks)
        for b in range(blocks):
            lanes = slice(b * LANES, (b + 1) * LANES)
            base_ref[q, 0, :, lanes] = middle[b][0]
            base_ref[q, 1, :, lanes] = middle[b][1]

    def table_rows(q, first):
        cols = []
        for b in range(blocks):
            lanes = slice(b * LANES, (b + 1) * LANES)
            bc, bs = base_ref[q, 0, :, lanes], base_ref[q, 1, :, lanes]
            up_c, up_s, down_c, down_s = [], [], [], []
            for d in range(first, first + PAIRS):
                at = 18 if d == 16 else d
                hc, hs = step_ref[0, at : at + 1, lanes], step_ref[1, at : at + 1, lanes]
                cc, ss, sc, cs = bc * hc, bs * hs, bs * hc, bc * hs
                up_c.append(bc if d == 16 else cc - ss)
                up_s.append(bs if d == 16 else sc + cs)
                down_c.append(cc + ss)
                down_s.append(sc - cs)
            cols.append(jnp.concatenate(up_c + up_s + down_c + down_s, axis=0).astype(bf16))
        return jnp.concatenate(cols, axis=1)

    for copy in copies:
        copy.wait()
    for q in range(SCOL):
        for first in range(1, 17, PAIRS):
            product = jnp.dot(table_rows(q, first), sky_ref[...], preferred_element_type=f32)
            side = 8 * PAIRS
            for k in range(2):
                c = product[2 * k * side : (2 * k + 1) * side]
                s = product[(2 * k + 1) * side : (2 * k + 2) * side]
                real = c[:, :LANES] + s[:, LANES:]
                imag = c[:, LANES:] - s[:, :LANES]
                for t in range(PAIRS):
                    d = first + t
                    group = 16 - d if k == 1 else 16 if d == 16 else 16 + d
                    rows = slice(8 * t, 8 * t + 8)
                    both = jnp.concatenate([real[rows], imag[rows]], axis=0)
                    out_ref[group, q * 16 : q * 16 + 16, :] = both.astype(bf16)


def first_axis(col_offsets, sky_re, sky_im):
    pixels = sky_re.shape[0]
    return pl.pallas_call(
        first_axis_kernel,
        in_specs=[HBM] * 3,
        out_specs=VMEM,
        out_shape=jax.ShapeDtypeStruct((32, 32, LANES), bf16),
        scratch_shapes=[
            pltpu.SMEM((SCOL,), jnp.int32),
            pltpu.VMEM((pixels, 2 * LANES), bf16),
            pltpu.VMEM((SCOL, 2, 8, pixels), f32),
            pltpu.VMEM((2, 24, pixels), f32),
            pltpu.SemaphoreType.DMA((1 + 2 * LOADS,)),
        ],
        compiler_params=WIDE,
        name="first_axis",
    )(col_offsets, sky_re, sky_im)


def table_parts(start, parts_ref):
    cells = lax.broadcasted_iota(jnp.int32, (8, S), 1)
    row = lax.broadcasted_iota(jnp.int32, (8, S), 0)
    for i, mult in enumerate((8 * row, 8 * row + 64, 8 * row + 128, row + 128)):
        scale = 1.0 / 256 if i == 3 else 1.0
        for k, phase in enumerate(cos_sin(mult * cells)):
            parts_ref[k, 8 * i : 8 * i + 8, :] = phase * scale
    for i in range(2):
        for k, phase in enumerate(cos_sin((start + 256 * (8 * i + row)) * cells)):
            parts_ref[k, 32 + 8 * i : 40 + 8 * i, :] = phase


def table_blocks(parts_ref, blocks):
    made = []
    for g in blocks:
        block = slice(32 + g, 33 + g)
        bc, bs = cmul(parts_ref[0, 24:32], parts_ref[1, 24:32], parts_ref[0, block], parts_ref[1, block])
        up, down = [], []
        for d in range(1, 17):
            hc, hs = parts_ref[0, d : d + 1], parts_ref[1, d : d + 1]
            cc, ss, sc, cs = bc * hc, bs * hs, bs * hc, bc * hs
            if d < 16:
                up.append(jnp.concatenate([cc - ss, sc + cs], axis=1))
            down.append(jnp.concatenate([cc + ss, sc - cs], axis=1))
        rows = down[::-1] + [jnp.concatenate([bc, bs], axis=1)] + up
        made.append(jnp.concatenate(rows, axis=0).astype(bf16))
    return made


def second_table_kernel(start_ref, sub_ref, table_ref, parts_ref, phases_ref):
    start = start_ref[0]
    table_parts(start, parts_ref)
    blocks = range(table_ref.shape[0] // 256)
    for g, made in zip(blocks, table_blocks(parts_ref, blocks)):
        table_ref[g * 256 : (g + 1) * 256, :] = made
    n_sub = sub_ref.shape[0]
    row = lax.broadcasted_iota(jnp.int32, (n_sub, LANES), 0)
    lane = lax.broadcasted_iota(jnp.int32, (n_sub, LANES), 1)
    offs = jnp.zeros((n_sub, LANES), jnp.int32)
    for s in range(n_sub):
        offs = jnp.where(row == s, sub_ref[s], offs)
    phases_ref[0], phases_ref[1] = cos_sin(offs * lane)
    phases_ref[2], phases_ref[3] = cos_sin(offs * (lane * LANES + start))


def second_table(start, sub_offsets, rows):
    return pl.pallas_call(
        second_table_kernel,
        in_specs=[SMEM, SMEM],
        out_specs=[VMEM] * 3,
        out_shape=[
            jax.ShapeDtypeStruct((rows, 2 * S), bf16),
            jax.ShapeDtypeStruct((2, 48, S), f32),
            jax.ShapeDtypeStruct((4, sub_offsets.shape[0], LANES), f32),
        ],
        compiler_params=PARAMS,
        name="second_table",
    )(start, sub_offsets)


def second_axis_kernel(band_ref, ready_ref, parts_ref, phases_ref, out_ref, shift_ref, table_ref):
    n_sub = phases_ref.shape[1]
    chunks = band_ref.shape[0]
    per = n_sub // SCOL
    ready = ready_ref.shape[0]
    low_c, low_s, high_c, high_s = (phases_ref[i] for i in range(4))
    for b in range(chunks):
        lanes = slice(b * LANES, (b + 1) * LANES)
        c, d = cmul(low_c, low_s, high_c[:, b : b + 1], high_s[:, b : b + 1])
        shift_ref[0, :, lanes] = c
        shift_ref[1, :, lanes] = d
    for g, made in enumerate(table_blocks(parts_ref, range(ready // 256, chunks // 2))):
        table_ref[g * 256 : (g + 1) * 256, :] = made

    def shifted(q):
        cols = []
        for c in range(chunks):
            lanes = slice(c * LANES, (c + 1) * LANES)
            band = band_ref[c, q * 16 : q * 16 + 16, :].astype(f32)
            re, im = band[:8], band[8:]
            rows = []
            for s in range(q * per, (q + 1) * per):
                mc = shift_ref[0, s : s + 1, lanes]
                md = shift_ref[1, s : s + 1, lanes]
                rows += [re * mc + im * md, im * mc - re * md]
            cols.append(jnp.concatenate(rows, axis=0).astype(bf16))
        return jnp.concatenate(cols, axis=1)

    left = jnp.concatenate([shifted(q) for q in range(SCOL)], axis=0)
    product = jnp.dot(left[:, :ready], ready_ref[...], preferred_element_type=f32)
    product = product + jnp.dot(left[:, ready:], table_ref[...], preferred_element_type=f32)
    product = product.reshape(n_sub, 16, 2 * S)
    re = product[:, :8, :S] + product[:, 8:, S:]
    im = product[:, 8:, :S] - product[:, :8, S:]
    out_ref[:, :S] = re.reshape(n_sub * 8, S).astype(bf16)
    out_ref[:, S:] = im.reshape(n_sub * 8, S).astype(bf16)


def second_axis(band, ready, parts, phases):
    n_sub = phases.shape[1]
    pixels = band.shape[0] * LANES
    return pl.pallas_call(
        second_axis_kernel,
        in_specs=[VMEM] * 4,
        out_specs=VMEM,
        out_shape=jax.ShapeDtypeStruct((n_sub * 8, 2 * S), bf16),
        scratch_shapes=[
            pltpu.VMEM((2, n_sub, pixels), f32),
            pltpu.VMEM((pixels - ready.shape[0], 2 * S), bf16),
        ],
        compiler_params=MIDDLE,
        name="second_axis",
    )(band, ready, parts, phases)


def own_rows_kernel(terms_ref, out_ref):
    total = terms_ref[0].astype(f32)
    for f in range(1, terms_ref.shape[0]):
        total = total + terms_ref[f].astype(f32)
    rows = total.astype(bf16)
    for c in range(out_ref.shape[0]):
        out_ref[c] = rows


def own_rows(terms, copies):
    return pl.pallas_call(
        own_rows_kernel,
        in_specs=[VMEM],
        out_specs=VMEM,
        out_shape=jax.ShapeDtypeStruct((copies, *terms.shape[1:]), bf16),
        compiler_params=PARAMS,
        name="own_rows",
    )(terms)


def weights_kernel(count_ref, kernel_ref, cell_ref, frac_ref, row_ref, col_ref):
    blocks, slots = cell_ref.shape[1:]
    for b in range(blocks):
        lanes = slice(b * slots, (b + 1) * slots)
        for axis in range(2):
            frac = frac_ref[axis, b : b + 1, :]
            ahead = lax.broadcasted_iota(jnp.int32, (S, slots), 0) - cell_ref[axis, b : b + 1, :]
            spread = jnp.zeros((S, slots), f32)
            for a in range(kernel_ref.shape[1]):
                tap = jnp.zeros((1, slots), f32)
                for o in range(kernel_ref.shape[0]):
                    tap = jnp.where(frac == o, kernel_ref[o, a], tap)
                spread = jnp.where(ahead == a, tap, spread)
            if axis == 0:
                live = lax.broadcasted_iota(jnp.int32, (1, slots), 1) < count_ref[b]
                row_ref[:, lanes] = jnp.where(live, spread, 0.0).astype(bf16)
            else:
                high = spread.astype(bf16)
                col_ref[:S, lanes] = high
                col_ref[S:, lanes] = (spread - high.astype(f32)).astype(bf16)


def weights(counts, kernel, cells, fracs):
    total = cells.shape[1] * cells.shape[2]
    return pl.pallas_call(
        weights_kernel,
        in_specs=[SMEM, SMEM, VMEM, VMEM],
        out_specs=[VMEM] * 2,
        out_shape=[jax.ShapeDtypeStruct((S, total), bf16), jax.ShapeDtypeStruct((2 * S, total), bf16)],
        compiler_params=PARAMS,
        name="weights",
    )(counts, kernel, cells, fracs)


def degrid_kernel(grid_ref, row_ref, col_ref, re_ref, im_ref):
    blocks, slots = re_ref.shape
    row = row_ref[...].astype(f32)
    cells = jnp.concatenate([grid_ref[:, :S], grid_ref[:, S:]], axis=0)
    sums = jnp.dot(jnp.concatenate([cells, cells], axis=1), col_ref[...], preferred_element_type=f32)
    for part, out_ref in ((0, re_ref), (1, im_ref)):
        values = jnp.sum(sums[part * S : (part + 1) * S] * row, axis=0, keepdims=True)
        for b in range(blocks):
            out_ref[b : b + 1, :] = values[:, b * slots : (b + 1) * slots]


def degrid(grid, row, col, blocks, slots):
    shape = jax.ShapeDtypeStruct((blocks, slots), f32)
    return pl.pallas_call(
        degrid_kernel,
        in_specs=[VMEM] * 3,
        out_specs=[VMEM] * 2,
        out_shape=[shape] * 2,
        compiler_params=PARAMS,
        name="degrid",
    )(grid, row, col)


def exchange(x, axis):
    return lax.all_to_all(x, axis, split_axis=0, concat_axis=0, tiled=True)


def local(sky_re, sky_im, col_offsets, sub_offsets, kernel, vis_count, cell_index, frac_index):
    pixels = sky_re.shape[1]
    n_sub = sub_offsets.shape[0]
    col = lax.axis_size("col")
    blocks, slots = cell_index.shape[2:]
    band = exchange(first_axis(col_offsets, sky_re[0], sky_im[0]), "col")
    start = (lax.axis_index("facet") * pixels).astype(jnp.int32).reshape(1)
    row, column = weights(vis_count[0], kernel, cell_index[:, 0], frac_index[:, 0])
    band, row, column = lax.optimization_barrier((band, row, column))
    terms = second_axis(band, *second_table(start, sub_offsets, READY))
    arrived = exchange(terms.reshape(n_sub, 8, 2 * S), "facet")
    grid = exchange(own_rows(arrived, col), "col").reshape(S, 2 * S)
    vis_re, vis_im = degrid(grid, row, column, blocks, slots)
    return vis_re[None], vis_im[None]


def solution(mesh):
    placed = (
        P("facet", None, "col"),
        P("facet", None, "col"),
        P(),
        P(),
        P(),
        P("facet", "col"),
        P(None, "facet", "col", None),
        P(None, "facet", "col", None),
    )
    return jax.shard_map(
        local,
        mesh=mesh,
        in_specs=placed,
        out_specs=(P("facet", "col", None), P("facet", "col", None)),
        check_vma=False,
    )
```

```python
import math

import jax
import jax.numpy as jnp
from jax import lax
from jax.experimental import pallas as pl
from jax.experimental.pallas import tpu as pltpu
from jax.sharding import PartitionSpec as P

N_IMG = 65536
S = 256
SCOL = 2
LANES = 128
PAIRS = 4
LOADS = 2
READY = 2304
PARAMS = pltpu.CompilerParams(vmem_limit_bytes=16 * 1024 * 1024)
MIDDLE = pltpu.CompilerParams(vmem_limit_bytes=24 * 1024 * 1024)
WIDE = pltpu.CompilerParams(vmem_limit_bytes=60 * 1024 * 1024)
VMEM = pl.BlockSpec(memory_space=pltpu.VMEM)
SMEM = pl.BlockSpec(memory_space=pltpu.SMEM)
HBM = pl.BlockSpec(memory_space=pltpu.HBM)
f32 = jnp.float32
bf16 = jnp.bfloat16


def cos_sin(p):
    q = (p + 8192) >> 14
    x = (p - (q << 14)).astype(f32) * (2.0 * math.pi / N_IMG)
    x2 = x * x
    s = x * (1.0 + x2 * (-1.0 / 6 + x2 * (1.0 / 120 + x2 * (-1.0 / 5040 + x2 * (1.0 / 362880)))))
    c = 1.0 + x2 * (-0.5 + x2 * (1.0 / 24 + x2 * (-1.0 / 720 + x2 * (1.0 / 40320))))
    odd = (q & 1) == 1
    a = jnp.where(odd, s, c)
    b = jnp.where(odd, c, s)
    return jnp.where(((q + 1) & 2) == 2, -a, a), jnp.where((q & 2) == 2, -b, b)


def cmul(ac, as_, bc, bs):
    return ac * bc - as_ * bs, as_ * bc + ac * bs


def row_phases(mult, scale, blocks):
    lane = lax.broadcasted_iota(jnp.int32, (8, LANES), 1)
    low_c, low_s = cos_sin(mult * lane)
    high_c, high_s = cos_sin(mult * (lane * LANES))
    low_c, low_s = low_c * scale, low_s * scale
    return [cmul(low_c, low_s, high_c[:, b : b + 1], high_s[:, b : b + 1]) for b in range(blocks)]


def first_axis_kernel(col_hbm, re_hbm, im_hbm, out_ref, col_ref, sky_ref, base_ref, step_ref, acc_ref, sem):
    pixels = re_hbm.shape[0]
    blocks = pixels // LANES
    part = pixels // LOADS
    col_copy = pltpu.make_async_copy(col_hbm, col_ref, sem.at[0])
    col_copy.start()
    copies = []
    for i in range(LOADS):
        for k, src in enumerate((re_hbm, im_hbm)):
            rows = pl.ds(i * part, part)
            dst = sky_ref.at[rows, pl.ds(k * LANES, LANES)]
            copies.append(pltpu.make_async_copy(src.at[rows], dst, sem.at[1 + 2 * i + k]))
            copies[-1].start()
    row = lax.broadcasted_iota(jnp.int32, (8, LANES), 0)
    near = row_phases(row * 8, 1.0, blocks)
    far = row_phases(row * 64, 1.0, blocks)
    for b in range(blocks):
        lanes = slice(b * LANES, (b + 1) * LANES)
        (near_c, near_s), (far_c, far_s) = near[b], far[b]
        next_c, next_s = cmul(near_c, near_s, far_c[1:2], far_s[1:2])
        for k, rows in enumerate(((near_c, next_c, far_c), (near_s, next_s, far_s))):
            for i in range(3):
                step_ref[k, 8 * i : 8 * i + 8, lanes] = rows[i]
    col_copy.wait()
    for q in range(SCOL):
        middle = row_phases(row + (col_ref[q] + 128), 1.0 / 64, blocks)
        for b in range(blocks):
            lanes = slice(b * LANES, (b + 1) * LANES)
            base_ref[q, 0, :, lanes] = middle[b][0]
            base_ref[q, 1, :, lanes] = middle[b][1]

    def table_rows(q, first, span):
        cols = []
        for b in span:
            lanes = slice(b * LANES, (b + 1) * LANES)
            bc, bs = base_ref[q, 0, :, lanes], base_ref[q, 1, :, lanes]
            up_c, up_s, down_c, down_s = [], [], [], []
            for d in range(first, first + PAIRS):
                at = 18 if d == 16 else d
                hc, hs = step_ref[0, at : at + 1, lanes], step_ref[1, at : at + 1, lanes]
                cc, ss, sc, cs = bc * hc, bs * hs, bs * hc, bc * hs
                up_c.append(bc if d == 16 else cc - ss)
                up_s.append(bs if d == 16 else sc + cs)
                down_c.append(cc + ss)
                down_s.append(sc - cs)
            cols.append(jnp.concatenate(up_c + up_s + down_c + down_s, axis=0).astype(bf16))
        return jnp.concatenate(cols, axis=1)

    groups = [(q, first) for q in range(SCOL) for first in range(1, 17, PAIRS)]
    for i in range(LOADS):
        copies[2 * i].wait()
        copies[2 * i + 1].wait()
        span = range(i * blocks // LOADS, (i + 1) * blocks // LOADS)
        pixel_rows = slice(i * part, (i + 1) * part)
        for at, (q, first) in enumerate(groups):
            product = jnp.dot(table_rows(q, first, span), sky_ref[pixel_rows, :], preferred_element_type=f32)
            if i > 0:
                product = product + acc_ref[at]
            if i < LOADS - 1:
                acc_ref[at] = product
                continue
            side = 8 * PAIRS
            for k in range(2):
                c = product[2 * k * side : (2 * k + 1) * side]
                s = product[(2 * k + 1) * side : (2 * k + 2) * side]
                real = c[:, :LANES] + s[:, LANES:]
                imag = c[:, LANES:] - s[:, :LANES]
                for t in range(PAIRS):
                    d = first + t
                    group = 16 - d if k == 1 else 16 if d == 16 else 16 + d
                    rows = slice(8 * t, 8 * t + 8)
                    both = jnp.concatenate([real[rows], imag[rows]], axis=0)
                    out_ref[group, q * 16 : q * 16 + 16, :] = both.astype(bf16)


def first_axis(col_offsets, sky_re, sky_im):
    pixels = sky_re.shape[0]
    return pl.pallas_call(
        first_axis_kernel,
        in_specs=[HBM] * 3,
        out_specs=VMEM,
        out_shape=jax.ShapeDtypeStruct((32, 32, LANES), bf16),
        scratch_shapes=[
            pltpu.SMEM((SCOL,), jnp.int32),
            pltpu.VMEM((pixels, 2 * LANES), bf16),
            pltpu.VMEM((SCOL, 2, 8, pixels), f32),
            pltpu.VMEM((2, 24, pixels), f32),
            pltpu.VMEM((32 // PAIRS, 32 * PAIRS, 2 * LANES), f32),
            pltpu.SemaphoreType.DMA((1 + 2 * LOADS,)),
        ],
        compiler_params=WIDE,
        name="first_axis",
    )(col_offsets, sky_re, sky_im)


def table_parts(start, parts_ref):
    cells = lax.broadcasted_iota(jnp.int32, (8, S), 1)
    row = lax.broadcasted_iota(jnp.int32, (8, S), 0)
    for i, mult in enumerate((8 * row, 8 * row + 64, 8 * row + 128, row + 128)):
        scale = 1.0 / 256 if i == 3 else 1.0
        for k, phase in enumerate(cos_sin(mult * cells)):
            parts_ref[k, 8 * i : 8 * i + 8, :] = phase * scale
    for i in range(2):
        for k, phase in enumerate(cos_sin((start + 256 * (8 * i + row)) * cells)):
            parts_ref[k, 32 + 8 * i : 40 + 8 * i, :] = phase


def table_blocks(parts_ref, blocks):
    made = []
    for g in blocks:
        block = slice(32 + g, 33 + g)
        bc, bs = cmul(parts_ref[0, 24:32], parts_ref[1, 24:32], parts_ref[0, block], parts_ref[1, block])
        up, down = [], []
        for d in range(1, 17):
            hc, hs = parts_ref[0, d : d + 1], parts_ref[1, d : d + 1]
            cc, ss, sc, cs = bc * hc, bs * hs, bs * hc, bc * hs
            if d < 16:
                up.append(jnp.concatenate([cc - ss, sc + cs], axis=1))
            down.append(jnp.concatenate([cc + ss, sc - cs], axis=1))
        rows = down[::-1] + [jnp.concatenate([bc, bs], axis=1)] + up
        made.append(jnp.concatenate(rows, axis=0).astype(bf16))
    return made


def second_table_kernel(start_ref, sub_ref, table_ref, parts_ref, phases_ref):
    start = start_ref[0]
    table_parts(start, parts_ref)
    blocks = range(table_ref.shape[0] // 256)
    for g, made in zip(blocks, table_blocks(parts_ref, blocks)):
        table_ref[g * 256 : (g + 1) * 256, :] = made
    n_sub = sub_ref.shape[0]
    row = lax.broadcasted_iota(jnp.int32, (n_sub, LANES), 0)
    lane = lax.broadcasted_iota(jnp.int32, (n_sub, LANES), 1)
    offs = jnp.zeros((n_sub, LANES), jnp.int32)
    for s in range(n_sub):
        offs = jnp.where(row == s, sub_ref[s], offs)
    phases_ref[0], phases_ref[1] = cos_sin(offs * lane)
    phases_ref[2], phases_ref[3] = cos_sin(offs * (lane * LANES + start))


def second_table(start, sub_offsets, rows):
    return pl.pallas_call(
        second_table_kernel,
        in_specs=[SMEM, SMEM],
        out_specs=[VMEM] * 3,
        out_shape=[
            jax.ShapeDtypeStruct((rows, 2 * S), bf16),
            jax.ShapeDtypeStruct((2, 48, S), f32),
            jax.ShapeDtypeStruct((4, sub_offsets.shape[0], LANES), f32),
        ],
        compiler_params=PARAMS,
        name="second_table",
    )(start, sub_offsets)


def second_axis_kernel(band_ref, ready_ref, parts_ref, phases_ref, out_ref, shift_ref, table_ref):
    n_sub = phases_ref.shape[1]
    chunks = band_ref.shape[0]
    per = n_sub // SCOL
    ready = ready_ref.shape[0]
    low_c, low_s, high_c, high_s = (phases_ref[i] for i in range(4))
    for b in range(chunks):
        lanes = slice(b * LANES, (b + 1) * LANES)
        c, d = cmul(low_c, low_s, high_c[:, b : b + 1], high_s[:, b : b + 1])
        shift_ref[0, :, lanes] = c
        shift_ref[1, :, lanes] = d
    for g, made in enumerate(table_blocks(parts_ref, range(ready // 256, chunks // 2))):
        table_ref[g * 256 : (g + 1) * 256, :] = made

    def shifted(q):
        cols = []
        for c in range(chunks):
            lanes = slice(c * LANES, (c + 1) * LANES)
            band = band_ref[c, q * 16 : q * 16 + 16, :].astype(f32)
            re, im = band[:8], band[8:]
            rows = []
            for s in range(q * per, (q + 1) * per):
                mc = shift_ref[0, s : s + 1, lanes]
                md = shift_ref[1, s : s + 1, lanes]
                rows += [re * mc + im * md, im * mc - re * md]
            cols.append(jnp.concatenate(rows, axis=0).astype(bf16))
        return jnp.concatenate(cols, axis=1)

    left = jnp.concatenate([shifted(q) for q in range(SCOL)], axis=0)
    product = jnp.dot(left[:, :ready], ready_ref[...], preferred_element_type=f32)
    product = product + jnp.dot(left[:, ready:], table_ref[...], preferred_element_type=f32)
    product = product.reshape(n_sub, 16, 2 * S)
    re = product[:, :8, :S] + product[:, 8:, S:]
    im = product[:, 8:, :S] - product[:, :8, S:]
    out_ref[:, :S] = re.reshape(n_sub * 8, S).astype(bf16)
    out_ref[:, S:] = im.reshape(n_sub * 8, S).astype(bf16)


def second_axis(band, ready, parts, phases):
    n_sub = phases.shape[1]
    pixels = band.shape[0] * LANES
    return pl.pallas_call(
        second_axis_kernel,
        in_specs=[VMEM] * 4,
        out_specs=VMEM,
        out_shape=jax.ShapeDtypeStruct((n_sub * 8, 2 * S), bf16),
        scratch_shapes=[
            pltpu.VMEM((2, n_sub, pixels), f32),
            pltpu.VMEM((pixels - ready.shape[0], 2 * S), bf16),
        ],
        compiler_params=MIDDLE,
        name="second_axis",
    )(band, ready, parts, phases)


def own_rows_kernel(terms_ref, out_ref):
    total = terms_ref[0].astype(f32)
    for f in range(1, terms_ref.shape[0]):
        total = total + terms_ref[f].astype(f32)
    rows = total.astype(bf16)
    for c in range(out_ref.shape[0]):
        out_ref[c] = rows


def own_rows(terms, copies):
    return pl.pallas_call(
        own_rows_kernel,
        in_specs=[VMEM],
        out_specs=VMEM,
        out_shape=jax.ShapeDtypeStruct((copies, *terms.shape[1:]), bf16),
        compiler_params=PARAMS,
        name="own_rows",
    )(terms)


def weights_kernel(count_ref, kernel_ref, cell_ref, frac_ref, row_ref, col_ref):
    blocks, slots = cell_ref.shape[1:]
    for b in range(blocks):
        lanes = slice(b * slots, (b + 1) * slots)
        for axis in range(2):
            frac = frac_ref[axis, b : b + 1, :]
            ahead = lax.broadcasted_iota(jnp.int32, (S, slots), 0) - cell_ref[axis, b : b + 1, :]
            spread = jnp.zeros((S, slots), f32)
            for a in range(kernel_ref.shape[1]):
                tap = jnp.zeros((1, slots), f32)
                for o in range(kernel_ref.shape[0]):
                    tap = jnp.where(frac == o, kernel_ref[o, a], tap)
                spread = jnp.where(ahead == a, tap, spread)
            if axis == 0:
                live = lax.broadcasted_iota(jnp.int32, (1, slots), 1) < count_ref[b]
                row_ref[:, lanes] = jnp.where(live, spread, 0.0).astype(bf16)
            else:
                high = spread.astype(bf16)
                col_ref[:S, lanes] = high
                col_ref[S:, lanes] = (spread - high.astype(f32)).astype(bf16)


def weights(counts, kernel, cells, fracs):
    total = cells.shape[1] * cells.shape[2]
    return pl.pallas_call(
        weights_kernel,
        in_specs=[SMEM, SMEM, VMEM, VMEM],
        out_specs=[VMEM] * 2,
        out_shape=[jax.ShapeDtypeStruct((S, total), bf16), jax.ShapeDtypeStruct((2 * S, total), bf16)],
        compiler_params=PARAMS,
        name="weights",
    )(counts, kernel, cells, fracs)


def degrid_kernel(grid_ref, row_ref, col_ref, re_ref, im_ref):
    blocks, slots = re_ref.shape
    row = row_ref[...].astype(f32)
    cells = jnp.concatenate([grid_ref[:, :S], grid_ref[:, S:]], axis=0)
    sums = jnp.dot(jnp.concatenate([cells, cells], axis=1), col_ref[...], preferred_element_type=f32)
    for part, out_ref in ((0, re_ref), (1, im_ref)):
        values = jnp.sum(sums[part * S : (part + 1) * S] * row, axis=0, keepdims=True)
        for b in range(blocks):
            out_ref[b : b + 1, :] = values[:, b * slots : (b + 1) * slots]


def degrid(grid, row, col, blocks, slots):
    shape = jax.ShapeDtypeStruct((blocks, slots), f32)
    return pl.pallas_call(
        degrid_kernel,
        in_specs=[VMEM] * 3,
        out_specs=[VMEM] * 2,
        out_shape=[shape] * 2,
        compiler_params=PARAMS,
        name="degrid",
    )(grid, row, col)


def exchange(x, axis):
    return lax.all_to_all(x, axis, split_axis=0, concat_axis=0, tiled=True)


def local(sky_re, sky_im, col_offsets, sub_offsets, kernel, vis_count, cell_index, frac_index):
    pixels = sky_re.shape[1]
    n_sub = sub_offsets.shape[0]
    col = lax.axis_size("col")
    blocks, slots = cell_index.shape[2:]
    band = exchange(first_axis(col_offsets, sky_re[0], sky_im[0]), "col")
    start = (lax.axis_index("facet") * pixels).astype(jnp.int32).reshape(1)
    row, column = weights(vis_count[0], kernel, cell_index[:, 0], frac_index[:, 0])
    band, row, column = lax.optimization_barrier((band, row, column))
    terms = second_axis(band, *second_table(start, sub_offsets, READY))
    arrived = exchange(terms.reshape(n_sub, 8, 2 * S), "facet")
    grid = exchange(own_rows(arrived, col), "col").reshape(S, 2 * S)
    vis_re, vis_im = degrid(grid, row, column, blocks, slots)
    return vis_re[None], vis_im[None]


def solution(mesh):
    placed = (
        P("facet", None, "col"),
        P("facet", None, "col"),
        P(),
        P(),
        P(),
        P("facet", "col"),
        P(None, "facet", "col", None),
        P(None, "facet", "col", None),
    )
    return jax.shard_map(
        local,
        mesh=mesh,
        in_specs=placed,
        out_specs=(P("facet", "col", None), P("facet", "col", None)),
        check_vma=False,
    )
```

```python
import math

import jax
import jax.numpy as jnp
from jax import lax
from jax.experimental import pallas as pl
from jax.experimental.pallas import tpu as pltpu
from jax.sharding import PartitionSpec as P

N_IMG = 65536
S = 256
SCOL = 2
LANES = 128
PAIRS = 4
LOADS = 4
READY = 2560
PARAMS = pltpu.CompilerParams(vmem_limit_bytes=16 * 1024 * 1024)
MIDDLE = pltpu.CompilerParams(vmem_limit_bytes=24 * 1024 * 1024)
WIDE = pltpu.CompilerParams(vmem_limit_bytes=60 * 1024 * 1024)
VMEM = pl.BlockSpec(memory_space=pltpu.VMEM)
SMEM = pl.BlockSpec(memory_space=pltpu.SMEM)
HBM = pl.BlockSpec(memory_space=pltpu.HBM)
f32 = jnp.float32
bf16 = jnp.bfloat16


def cos_sin(p):
    q = (p + 8192) >> 14
    x = (p - (q << 14)).astype(f32) * (2.0 * math.pi / N_IMG)
    x2 = x * x
    s = x * (1.0 + x2 * (-1.0 / 6 + x2 * (1.0 / 120 + x2 * (-1.0 / 5040 + x2 * (1.0 / 362880)))))
    c = 1.0 + x2 * (-0.5 + x2 * (1.0 / 24 + x2 * (-1.0 / 720 + x2 * (1.0 / 40320))))
    odd = (q & 1) == 1
    a = jnp.where(odd, s, c)
    b = jnp.where(odd, c, s)
    return jnp.where(((q + 1) & 2) == 2, -a, a), jnp.where((q & 2) == 2, -b, b)


def cmul(ac, as_, bc, bs):
    return ac * bc - as_ * bs, as_ * bc + ac * bs


def row_phases(mult, scale, blocks):
    lane = lax.broadcasted_iota(jnp.int32, (8, LANES), 1)
    low_c, low_s = cos_sin(mult * lane)
    high_c, high_s = cos_sin(mult * (lane * LANES))
    low_c, low_s = low_c * scale, low_s * scale
    return [cmul(low_c, low_s, high_c[:, b : b + 1], high_s[:, b : b + 1]) for b in range(blocks)]


def first_axis_kernel(col_hbm, re_hbm, im_hbm, out_ref, col_ref, sky_ref, base_ref, step_ref, acc_ref, sem):
    pixels = re_hbm.shape[0]
    blocks = pixels // LANES
    part = pixels // LOADS
    col_copy = pltpu.make_async_copy(col_hbm, col_ref, sem.at[0])
    col_copy.start()
    copies = []
    for i in range(LOADS):
        for k, src in enumerate((re_hbm, im_hbm)):
            rows = pl.ds(i * part, part)
            dst = sky_ref.at[rows, pl.ds(k * LANES, LANES)]
            copies.append(pltpu.make_async_copy(src.at[rows], dst, sem.at[1 + 2 * i + k]))
            copies[-1].start()
    row = lax.broadcasted_iota(jnp.int32, (8, LANES), 0)
    near = row_phases(row * 8, 1.0, blocks)
    far = row_phases(row * 64, 1.0, blocks)
    for b in range(blocks):
        lanes = slice(b * LANES, (b + 1) * LANES)
        (near_c, near_s), (far_c, far_s) = near[b], far[b]
        next_c, next_s = cmul(near_c, near_s, far_c[1:2], far_s[1:2])
        for k, rows in enumerate(((near_c, next_c, far_c), (near_s, next_s, far_s))):
            for i in range(3):
                step_ref[k, 8 * i : 8 * i + 8, lanes] = rows[i]
    col_copy.wait()
    for q in range(SCOL):
        middle = row_phases(row + (col_ref[q] + 128), 1.0 / 64, blocks)
        for b in range(blocks):
            lanes = slice(b * LANES, (b + 1) * LANES)
            base_ref[q, 0, :, lanes] = middle[b][0]
            base_ref[q, 1, :, lanes] = middle[b][1]

    def table_rows(q, first, span):
        cols = []
        for b in span:
            lanes = slice(b * LANES, (b + 1) * LANES)
            bc, bs = base_ref[q, 0, :, lanes], base_ref[q, 1, :, lanes]
            up_c, up_s, down_c, down_s = [], [], [], []
            for d in range(first, first + PAIRS):
                at = 18 if d == 16 else d
                hc, hs = step_ref[0, at : at + 1, lanes], step_ref[1, at : at + 1, lanes]
                cc, ss, sc, cs = bc * hc, bs * hs, bs * hc, bc * hs
                up_c.append(bc if d == 16 else cc - ss)
                up_s.append(bs if d == 16 else sc + cs)
                down_c.append(cc + ss)
                down_s.append(sc - cs)
            cols.append(jnp.concatenate(up_c + up_s + down_c + down_s, axis=0).astype(bf16))
        return jnp.concatenate(cols, axis=1)

    groups = [(q, first) for q in range(SCOL) for first in range(1, 17, PAIRS)]
    for i in range(LOADS):
        copies[2 * i].wait()
        copies[2 * i + 1].wait()
        span = range(i * blocks // LOADS, (i + 1) * blocks // LOADS)
        pixel_rows = slice(i * part, (i + 1) * part)
        for at, (q, first) in enumerate(groups):
            product = jnp.dot(table_rows(q, first, span), sky_ref[pixel_rows, :], preferred_element_type=f32)
            if i > 0:
                product = product + acc_ref[at]
            if i < LOADS - 1:
                acc_ref[at] = product
                continue
            side = 8 * PAIRS
            for k in range(2):
                c = product[2 * k * side : (2 * k + 1) * side]
                s = product[(2 * k + 1) * side : (2 * k + 2) * side]
                real = c[:, :LANES] + s[:, LANES:]
                imag = c[:, LANES:] - s[:, :LANES]
                for t in range(PAIRS):
                    d = first + t
                    group = 16 - d if k == 1 else 16 if d == 16 else 16 + d
                    rows = slice(8 * t, 8 * t + 8)
                    both = jnp.concatenate([real[rows], imag[rows]], axis=0)
                    out_ref[group, q * 16 : q * 16 + 16, :] = both.astype(bf16)


def first_axis(col_offsets, sky_re, sky_im):
    pixels = sky_re.shape[0]
    return pl.pallas_call(
        first_axis_kernel,
        in_specs=[HBM] * 3,
        out_specs=VMEM,
        out_shape=jax.ShapeDtypeStruct((32, 32, LANES), bf16),
        scratch_shapes=[
            pltpu.SMEM((SCOL,), jnp.int32),
            pltpu.VMEM((pixels, 2 * LANES), bf16),
            pltpu.VMEM((SCOL, 2, 8, pixels), f32),
            pltpu.VMEM((2, 24, pixels), f32),
            pltpu.VMEM((32 // PAIRS, 32 * PAIRS, 2 * LANES), f32),
            pltpu.SemaphoreType.DMA((1 + 2 * LOADS,)),
        ],
        compiler_params=WIDE,
        name="first_axis",
    )(col_offsets, sky_re, sky_im)


def table_parts(start, parts_ref):
    cells = lax.broadcasted_iota(jnp.int32, (8, S), 1)
    row = lax.broadcasted_iota(jnp.int32, (8, S), 0)
    for i, mult in enumerate((8 * row, 8 * row + 64, 8 * row + 128, row + 128)):
        scale = 1.0 / 256 if i == 3 else 1.0
        for k, phase in enumerate(cos_sin(mult * cells)):
            parts_ref[k, 8 * i : 8 * i + 8, :] = phase * scale
    for i in range(2):
        for k, phase in enumerate(cos_sin((start + 256 * (8 * i + row)) * cells)):
            parts_ref[k, 32 + 8 * i : 40 + 8 * i, :] = phase


def table_blocks(parts_ref, blocks):
    made = []
    for g in blocks:
        block = slice(32 + g, 33 + g)
        bc, bs = cmul(parts_ref[0, 24:32], parts_ref[1, 24:32], parts_ref[0, block], parts_ref[1, block])
        up, down = [], []
        for d in range(1, 17):
            hc, hs = parts_ref[0, d : d + 1], parts_ref[1, d : d + 1]
            cc, ss, sc, cs = bc * hc, bs * hs, bs * hc, bc * hs
            if d < 16:
                up.append(jnp.concatenate([cc - ss, sc + cs], axis=1))
            down.append(jnp.concatenate([cc + ss, sc - cs], axis=1))
        rows = down[::-1] + [jnp.concatenate([bc, bs], axis=1)] + up
        made.append(jnp.concatenate(rows, axis=0).astype(bf16))
    return made


def second_table_kernel(start_ref, sub_ref, table_ref, parts_ref, phases_ref):
    start = start_ref[0]
    table_parts(start, parts_ref)
    blocks = range(table_ref.shape[0] // 256)
    for g, made in zip(blocks, table_blocks(parts_ref, blocks)):
        table_ref[g * 256 : (g + 1) * 256, :] = made
    n_sub = sub_ref.shape[0]
    row = lax.broadcasted_iota(jnp.int32, (n_sub, LANES), 0)
    lane = lax.broadcasted_iota(jnp.int32, (n_sub, LANES), 1)
    offs = jnp.zeros((n_sub, LANES), jnp.int32)
    for s in range(n_sub):
        offs = jnp.where(row == s, sub_ref[s], offs)
    phases_ref[0], phases_ref[1] = cos_sin(offs * lane)
    phases_ref[2], phases_ref[3] = cos_sin(offs * (lane * LANES + start))


def second_table(start, sub_offsets, rows):
    return pl.pallas_call(
        second_table_kernel,
        in_specs=[SMEM, SMEM],
        out_specs=[VMEM] * 3,
        out_shape=[
            jax.ShapeDtypeStruct((rows, 2 * S), bf16),
            jax.ShapeDtypeStruct((2, 48, S), f32),
            jax.ShapeDtypeStruct((4, sub_offsets.shape[0], LANES), f32),
        ],
        compiler_params=PARAMS,
        name="second_table",
    )(start, sub_offsets)


def second_axis_kernel(band_ref, ready_ref, parts_ref, phases_ref, out_ref, shift_ref, table_ref):
    n_sub = phases_ref.shape[1]
    chunks = band_ref.shape[0]
    per = n_sub // SCOL
    ready = ready_ref.shape[0]
    low_c, low_s, high_c, high_s = (phases_ref[i] for i in range(4))
    for b in range(chunks):
        lanes = slice(b * LANES, (b + 1) * LANES)
        c, d = cmul(low_c, low_s, high_c[:, b : b + 1], high_s[:, b : b + 1])
        shift_ref[0, :, lanes] = c
        shift_ref[1, :, lanes] = d
    for g, made in enumerate(table_blocks(parts_ref, range(ready // 256, chunks // 2))):
        table_ref[g * 256 : (g + 1) * 256, :] = made

    def shifted(q):
        cols = []
        for c in range(chunks):
            lanes = slice(c * LANES, (c + 1) * LANES)
            band = band_ref[c, q * 16 : q * 16 + 16, :].astype(f32)
            re, im = band[:8], band[8:]
            rows = []
            for s in range(q * per, (q + 1) * per):
                mc = shift_ref[0, s : s + 1, lanes]
                md = shift_ref[1, s : s + 1, lanes]
                rows += [re * mc + im * md, im * mc - re * md]
            cols.append(jnp.concatenate(rows, axis=0).astype(bf16))
        return jnp.concatenate(cols, axis=1)

    left = jnp.concatenate([shifted(q) for q in range(SCOL)], axis=0)
    product = jnp.dot(left[:, :ready], ready_ref[...], preferred_element_type=f32)
    product = product + jnp.dot(left[:, ready:], table_ref[...], preferred_element_type=f32)
    product = product.reshape(n_sub, 16, 2 * S)
    re = product[:, :8, :S] + product[:, 8:, S:]
    im = product[:, 8:, :S] - product[:, :8, S:]
    out_ref[:, :S] = re.reshape(n_sub * 8, S).astype(bf16)
    out_ref[:, S:] = im.reshape(n_sub * 8, S).astype(bf16)


def second_axis(band, ready, parts, phases):
    n_sub = phases.shape[1]
    pixels = band.shape[0] * LANES
    return pl.pallas_call(
        second_axis_kernel,
        in_specs=[VMEM] * 4,
        out_specs=VMEM,
        out_shape=jax.ShapeDtypeStruct((n_sub * 8, 2 * S), bf16),
        scratch_shapes=[
            pltpu.VMEM((2, n_sub, pixels), f32),
            pltpu.VMEM((pixels - ready.shape[0], 2 * S), bf16),
        ],
        compiler_params=MIDDLE,
        name="second_axis",
    )(band, ready, parts, phases)


def own_rows_kernel(terms_ref, out_ref):
    total = terms_ref[0].astype(f32)
    for f in range(1, terms_ref.shape[0]):
        total = total + terms_ref[f].astype(f32)
    rows = total.astype(bf16)
    for c in range(out_ref.shape[0]):
        out_ref[c] = rows


def own_rows(terms, copies):
    return pl.pallas_call(
        own_rows_kernel,
        in_specs=[VMEM],
        out_specs=VMEM,
        out_shape=jax.ShapeDtypeStruct((copies, *terms.shape[1:]), bf16),
        compiler_params=PARAMS,
        name="own_rows",
    )(terms)


def weights_kernel(count_ref, kernel_ref, cell_ref, frac_ref, row_ref, col_ref):
    blocks, slots = cell_ref.shape[1:]
    for b in range(blocks):
        lanes = slice(b * slots, (b + 1) * slots)
        for axis in range(2):
            frac = frac_ref[axis, b : b + 1, :]
            ahead = lax.broadcasted_iota(jnp.int32, (S, slots), 0) - cell_ref[axis, b : b + 1, :]
            spread = jnp.zeros((S, slots), f32)
            for a in range(kernel_ref.shape[1]):
                tap = jnp.zeros((1, slots), f32)
                for o in range(kernel_ref.shape[0]):
                    tap = jnp.where(frac == o, kernel_ref[o, a], tap)
                spread = jnp.where(ahead == a, tap, spread)
            if axis == 0:
                live = lax.broadcasted_iota(jnp.int32, (1, slots), 1) < count_ref[b]
                row_ref[:, lanes] = jnp.where(live, spread, 0.0).astype(bf16)
            else:
                high = spread.astype(bf16)
                col_ref[:S, lanes] = high
                col_ref[S:, lanes] = (spread - high.astype(f32)).astype(bf16)


def weights(counts, kernel, cells, fracs):
    total = cells.shape[1] * cells.shape[2]
    return pl.pallas_call(
        weights_kernel,
        in_specs=[SMEM, SMEM, VMEM, VMEM],
        out_specs=[VMEM] * 2,
        out_shape=[jax.ShapeDtypeStruct((S, total), bf16), jax.ShapeDtypeStruct((2 * S, total), bf16)],
        compiler_params=PARAMS,
        name="weights",
    )(counts, kernel, cells, fracs)


def degrid_kernel(grid_ref, row_ref, col_ref, re_ref, im_ref):
    blocks, slots = re_ref.shape
    row = row_ref[...].astype(f32)
    cells = jnp.concatenate([grid_ref[:, :S], grid_ref[:, S:]], axis=0)
    sums = jnp.dot(jnp.concatenate([cells, cells], axis=1), col_ref[...], preferred_element_type=f32)
    for part, out_ref in ((0, re_ref), (1, im_ref)):
        values = jnp.sum(sums[part * S : (part + 1) * S] * row, axis=0, keepdims=True)
        for b in range(blocks):
            out_ref[b : b + 1, :] = values[:, b * slots : (b + 1) * slots]


def degrid(grid, row, col, blocks, slots):
    shape = jax.ShapeDtypeStruct((blocks, slots), f32)
    return pl.pallas_call(
        degrid_kernel,
        in_specs=[VMEM] * 3,
        out_specs=[VMEM] * 2,
        out_shape=[shape] * 2,
        compiler_params=PARAMS,
        name="degrid",
    )(grid, row, col)


def exchange(x, axis):
    return lax.all_to_all(x, axis, split_axis=0, concat_axis=0, tiled=True)


def local(sky_re, sky_im, col_offsets, sub_offsets, kernel, vis_count, cell_index, frac_index):
    pixels = sky_re.shape[1]
    n_sub = sub_offsets.shape[0]
    col = lax.axis_size("col")
    blocks, slots = cell_index.shape[2:]
    band = exchange(first_axis(col_offsets, sky_re[0], sky_im[0]), "col")
    start = (lax.axis_index("facet") * pixels).astype(jnp.int32).reshape(1)
    row, column = weights(vis_count[0], kernel, cell_index[:, 0], frac_index[:, 0])
    band, row, column = lax.optimization_barrier((band, row, column))
    terms = second_axis(band, *second_table(start, sub_offsets, READY))
    arrived = exchange(terms.reshape(n_sub, 8, 2 * S), "facet")
    grid = exchange(own_rows(arrived, col), "col").reshape(S, 2 * S)
    vis_re, vis_im = degrid(grid, row, column, blocks, slots)
    return vis_re[None], vis_im[None]


def solution(mesh):
    placed = (
        P("facet", None, "col"),
        P("facet", None, "col"),
        P(),
        P(),
        P(),
        P("facet", "col"),
        P(None, "facet", "col", None),
        P(None, "facet", "col", None),
    )
    return jax.shard_map(
        local,
        mesh=mesh,
        in_specs=placed,
        out_specs=(P("facet", "col", None), P("facet", "col", None)),
        check_vma=False,
    )
```

```python
import math

import jax
import jax.numpy as jnp
from jax import lax
from jax.experimental import pallas as pl
from jax.experimental.pallas import tpu as pltpu
from jax.sharding import PartitionSpec as P

N_IMG = 65536
S = 256
SCOL = 2
LANES = 128
PAIRS = 4
LOADS = 2
READY = 2304
PARAMS = pltpu.CompilerParams(vmem_limit_bytes=16 * 1024 * 1024)
MIDDLE = pltpu.CompilerParams(vmem_limit_bytes=24 * 1024 * 1024)
WIDE = pltpu.CompilerParams(vmem_limit_bytes=60 * 1024 * 1024)
VMEM = pl.BlockSpec(memory_space=pltpu.VMEM)
SMEM = pl.BlockSpec(memory_space=pltpu.SMEM)
HBM = pl.BlockSpec(memory_space=pltpu.HBM)
f32 = jnp.float32
bf16 = jnp.bfloat16


def cos_sin(p):
    q = (p + 8192) >> 14
    x = (p - (q << 14)).astype(f32) * (2.0 * math.pi / N_IMG)
    x2 = x * x
    s = x * (1.0 + x2 * (-1.0 / 6 + x2 * (1.0 / 120 + x2 * (-1.0 / 5040 + x2 * (1.0 / 362880)))))
    c = 1.0 + x2 * (-0.5 + x2 * (1.0 / 24 + x2 * (-1.0 / 720 + x2 * (1.0 / 40320))))
    odd = (q & 1) == 1
    a = jnp.where(odd, s, c)
    b = jnp.where(odd, c, s)
    return jnp.where(((q + 1) & 2) == 2, -a, a), jnp.where((q & 2) == 2, -b, b)


def cmul(ac, as_, bc, bs):
    return ac * bc - as_ * bs, as_ * bc + ac * bs


def row_phases(mult, scale, blocks):
    lane = lax.broadcasted_iota(jnp.int32, (8, LANES), 1)
    low_c, low_s = cos_sin(mult * lane)
    high_c, high_s = cos_sin(mult * (lane * LANES))
    low_c, low_s = low_c * scale, low_s * scale
    return [cmul(low_c, low_s, high_c[:, b : b + 1], high_s[:, b : b + 1]) for b in range(blocks)]


def first_axis_kernel(col_hbm, re_hbm, im_hbm, out_hbm, col_ref, sky_ref, base_ref, step_ref, acc_ref, stage_ref, sem):
    pixels = re_hbm.shape[0]
    blocks = pixels // LANES
    part = pixels // LOADS
    col_copy = pltpu.make_async_copy(col_hbm, col_ref, sem.at[0])
    col_copy.start()
    copies = []
    for i in range(LOADS):
        for k, src in enumerate((re_hbm, im_hbm)):
            rows = pl.ds(i * part, part)
            dst = sky_ref.at[rows, pl.ds(k * LANES, LANES)]
            copies.append(pltpu.make_async_copy(src.at[rows], dst, sem.at[1 + 2 * i + k]))
            copies[-1].start()
    row = lax.broadcasted_iota(jnp.int32, (8, LANES), 0)
    near = row_phases(row * 8, 1.0, blocks)
    far = row_phases(row * 64, 1.0, blocks)
    for b in range(blocks):
        lanes = slice(b * LANES, (b + 1) * LANES)
        (near_c, near_s), (far_c, far_s) = near[b], far[b]
        next_c, next_s = cmul(near_c, near_s, far_c[1:2], far_s[1:2])
        for k, rows in enumerate(((near_c, next_c, far_c), (near_s, next_s, far_s))):
            for i in range(3):
                step_ref[k, 8 * i : 8 * i + 8, lanes] = rows[i]
    col_copy.wait()
    for q in range(SCOL):
        middle = row_phases(row + (col_ref[q] + 128), 1.0 / 64, blocks)
        for b in range(blocks):
            lanes = slice(b * LANES, (b + 1) * LANES)
            base_ref[q, 0, :, lanes] = middle[b][0]
            base_ref[q, 1, :, lanes] = middle[b][1]

    def table_rows(q, first, span):
        cols = []
        for b in span:
            lanes = slice(b * LANES, (b + 1) * LANES)
            bc, bs = base_ref[q, 0, :, lanes], base_ref[q, 1, :, lanes]
            up_c, up_s, down_c, down_s = [], [], [], []
            for d in range(first, first + PAIRS):
                at = 18 if d == 16 else d
                hc, hs = step_ref[0, at : at + 1, lanes], step_ref[1, at : at + 1, lanes]
                cc, ss, sc, cs = bc * hc, bs * hs, bs * hc, bc * hs
                up_c.append(bc if d == 16 else cc - ss)
                up_s.append(bs if d == 16 else sc + cs)
                down_c.append(cc + ss)
                down_s.append(sc - cs)
            cols.append(jnp.concatenate(up_c + up_s + down_c + down_s, axis=0).astype(bf16))
        return jnp.concatenate(cols, axis=1)

    sent = []
    groups = [(q, first) for q in range(SCOL) for first in range(1, 17, PAIRS)]
    for i in range(LOADS):
        copies[2 * i].wait()
        copies[2 * i + 1].wait()
        span = range(i * blocks // LOADS, (i + 1) * blocks // LOADS)
        pixel_rows = slice(i * part, (i + 1) * part)
        for at, (q, first) in enumerate(groups):
            product = jnp.dot(table_rows(q, first, span), sky_ref[pixel_rows, :], preferred_element_type=f32)
            if i > 0:
                product = product + acc_ref[at]
            if i < LOADS - 1:
                acc_ref[at] = product
                continue
            side = 8 * PAIRS
            for k in range(2):
                c = product[2 * k * side : (2 * k + 1) * side]
                s = product[(2 * k + 1) * side : (2 * k + 2) * side]
                real = c[:, :LANES] + s[:, LANES:]
                imag = c[:, LANES:] - s[:, :LANES]
                for t in range(PAIRS):
                    d = first + t
                    group = 16 - d if k == 1 else 16 if d == 16 else 16 + d
                    rows = slice(8 * t, 8 * t + 8)
                    both = jnp.concatenate([real[rows], imag[rows]], axis=0)
                    stage_ref[group, q * 16 : q * 16 + 16, :] = both.astype(bf16)
            if first + PAIRS > 16:
                rows = pl.ds(q * 16, 16)
                out_copy = pltpu.make_async_copy(stage_ref.at[:, rows], out_hbm.at[:, rows], sem.at[1 + 2 * LOADS + q])
                out_copy.start()
                sent.append(out_copy)
    for copy in sent:
        copy.wait()


def first_axis(col_offsets, sky_re, sky_im):
    pixels = sky_re.shape[0]
    return pl.pallas_call(
        first_axis_kernel,
        in_specs=[HBM] * 3,
        out_specs=HBM,
        out_shape=jax.ShapeDtypeStruct((32, 32, LANES), bf16),
        scratch_shapes=[
            pltpu.SMEM((SCOL,), jnp.int32),
            pltpu.VMEM((pixels, 2 * LANES), bf16),
            pltpu.VMEM((SCOL, 2, 8, pixels), f32),
            pltpu.VMEM((2, 24, pixels), f32),
            pltpu.VMEM((32 // PAIRS, 32 * PAIRS, 2 * LANES), f32),
            pltpu.VMEM((32, 32, LANES), bf16),
            pltpu.SemaphoreType.DMA((1 + 2 * LOADS + SCOL,)),
        ],
        compiler_params=WIDE,
        name="first_axis",
    )(col_offsets, sky_re, sky_im)


def table_parts(start, parts_ref):
    cells = lax.broadcasted_iota(jnp.int32, (8, S), 1)
    row = lax.broadcasted_iota(jnp.int32, (8, S), 0)
    for i, mult in enumerate((8 * row, 8 * row + 64, 8 * row + 128, row + 128)):
        scale = 1.0 / 256 if i == 3 else 1.0
        for k, phase in enumerate(cos_sin(mult * cells)):
            parts_ref[k, 8 * i : 8 * i + 8, :] = phase * scale
    for i in range(2):
        for k, phase in enumerate(cos_sin((start + 256 * (8 * i + row)) * cells)):
            parts_ref[k, 32 + 8 * i : 40 + 8 * i, :] = phase


def table_blocks(parts_ref, blocks):
    made = []
    for g in blocks:
        block = slice(32 + g, 33 + g)
        bc, bs = cmul(parts_ref[0, 24:32], parts_ref[1, 24:32], parts_ref[0, block], parts_ref[1, block])
        up, down = [], []
        for d in range(1, 17):
            hc, hs = parts_ref[0, d : d + 1], parts_ref[1, d : d + 1]
            cc, ss, sc, cs = bc * hc, bs * hs, bs * hc, bc * hs
            if d < 16:
                up.append(jnp.concatenate([cc - ss, sc + cs], axis=1))
            down.append(jnp.concatenate([cc + ss, sc - cs], axis=1))
        rows = down[::-1] + [jnp.concatenate([bc, bs], axis=1)] + up
        made.append(jnp.concatenate(rows, axis=0).astype(bf16))
    return made


def second_table_kernel(start_ref, sub_ref, table_ref, parts_ref, phases_ref):
    start = start_ref[0]
    table_parts(start, parts_ref)
    blocks = range(table_ref.shape[0] // 256)
    for g, made in zip(blocks, table_blocks(parts_ref, blocks)):
        table_ref[g * 256 : (g + 1) * 256, :] = made
    n_sub = sub_ref.shape[0]
    row = lax.broadcasted_iota(jnp.int32, (n_sub, LANES), 0)
    lane = lax.broadcasted_iota(jnp.int32, (n_sub, LANES), 1)
    offs = jnp.zeros((n_sub, LANES), jnp.int32)
    for s in range(n_sub):
        offs = jnp.where(row == s, sub_ref[s], offs)
    phases_ref[0], phases_ref[1] = cos_sin(offs * lane)
    phases_ref[2], phases_ref[3] = cos_sin(offs * (lane * LANES + start))


def second_table(start, sub_offsets, rows):
    return pl.pallas_call(
        second_table_kernel,
        in_specs=[SMEM, SMEM],
        out_specs=[VMEM] * 3,
        out_shape=[
            jax.ShapeDtypeStruct((rows, 2 * S), bf16),
            jax.ShapeDtypeStruct((2, 48, S), f32),
            jax.ShapeDtypeStruct((4, sub_offsets.shape[0], LANES), f32),
        ],
        compiler_params=PARAMS,
        name="second_table",
    )(start, sub_offsets)


def second_axis_kernel(band_ref, ready_ref, parts_ref, phases_ref, out_ref, shift_ref, table_ref):
    n_sub = phases_ref.shape[1]
    chunks = band_ref.shape[0]
    per = n_sub // SCOL
    ready = ready_ref.shape[0]
    low_c, low_s, high_c, high_s = (phases_ref[i] for i in range(4))
    for b in range(chunks):
        lanes = slice(b * LANES, (b + 1) * LANES)
        c, d = cmul(low_c, low_s, high_c[:, b : b + 1], high_s[:, b : b + 1])
        shift_ref[0, :, lanes] = c
        shift_ref[1, :, lanes] = d
    for g, made in enumerate(table_blocks(parts_ref, range(ready // 256, chunks // 2))):
        table_ref[g * 256 : (g + 1) * 256, :] = made

    def shifted(q):
        cols = []
        for c in range(chunks):
            lanes = slice(c * LANES, (c + 1) * LANES)
            band = band_ref[c, q * 16 : q * 16 + 16, :].astype(f32)
            re, im = band[:8], band[8:]
            rows = []
            for s in range(q * per, (q + 1) * per):
                mc = shift_ref[0, s : s + 1, lanes]
                md = shift_ref[1, s : s + 1, lanes]
                rows += [re * mc + im * md, im * mc - re * md]
            cols.append(jnp.concatenate(rows, axis=0).astype(bf16))
        return jnp.concatenate(cols, axis=1)

    left = jnp.concatenate([shifted(q) for q in range(SCOL)], axis=0)
    product = jnp.dot(left[:, :ready], ready_ref[...], preferred_element_type=f32)
    product = product + jnp.dot(left[:, ready:], table_ref[...], preferred_element_type=f32)
    product = product.reshape(n_sub, 16, 2 * S)
    re = product[:, :8, :S] + product[:, 8:, S:]
    im = product[:, 8:, :S] - product[:, :8, S:]
    out_ref[:, :S] = re.reshape(n_sub * 8, S).astype(bf16)
    out_ref[:, S:] = im.reshape(n_sub * 8, S).astype(bf16)


def second_axis(band, ready, parts, phases):
    n_sub = phases.shape[1]
    pixels = band.shape[0] * LANES
    return pl.pallas_call(
        second_axis_kernel,
        in_specs=[VMEM] * 4,
        out_specs=VMEM,
        out_shape=jax.ShapeDtypeStruct((n_sub * 8, 2 * S), bf16),
        scratch_shapes=[
            pltpu.VMEM((2, n_sub, pixels), f32),
            pltpu.VMEM((pixels - ready.shape[0], 2 * S), bf16),
        ],
        compiler_params=MIDDLE,
        name="second_axis",
    )(band, ready, parts, phases)


def own_rows_kernel(terms_ref, out_ref):
    total = terms_ref[0].astype(f32)
    for f in range(1, terms_ref.shape[0]):
        total = total + terms_ref[f].astype(f32)
    rows = total.astype(bf16)
    for c in range(out_ref.shape[0]):
        out_ref[c] = rows


def own_rows(terms, copies):
    return pl.pallas_call(
        own_rows_kernel,
        in_specs=[VMEM],
        out_specs=VMEM,
        out_shape=jax.ShapeDtypeStruct((copies, *terms.shape[1:]), bf16),
        compiler_params=PARAMS,
        name="own_rows",
    )(terms)


def weights_kernel(count_ref, kernel_ref, cell_ref, frac_ref, row_ref, col_ref):
    blocks, slots = cell_ref.shape[1:]
    for b in range(blocks):
        lanes = slice(b * slots, (b + 1) * slots)
        for axis in range(2):
            frac = frac_ref[axis, b : b + 1, :]
            ahead = lax.broadcasted_iota(jnp.int32, (S, slots), 0) - cell_ref[axis, b : b + 1, :]
            spread = jnp.zeros((S, slots), f32)
            for a in range(kernel_ref.shape[1]):
                tap = jnp.zeros((1, slots), f32)
                for o in range(kernel_ref.shape[0]):
                    tap = jnp.where(frac == o, kernel_ref[o, a], tap)
                spread = jnp.where(ahead == a, tap, spread)
            if axis == 0:
                live = lax.broadcasted_iota(jnp.int32, (1, slots), 1) < count_ref[b]
                row_ref[:, lanes] = jnp.where(live, spread, 0.0).astype(bf16)
            else:
                high = spread.astype(bf16)
                col_ref[:S, lanes] = high
                col_ref[S:, lanes] = (spread - high.astype(f32)).astype(bf16)


def weights(counts, kernel, cells, fracs):
    total = cells.shape[1] * cells.shape[2]
    return pl.pallas_call(
        weights_kernel,
        in_specs=[SMEM, SMEM, VMEM, VMEM],
        out_specs=[VMEM] * 2,
        out_shape=[jax.ShapeDtypeStruct((S, total), bf16), jax.ShapeDtypeStruct((2 * S, total), bf16)],
        compiler_params=PARAMS,
        name="weights",
    )(counts, kernel, cells, fracs)


def degrid_kernel(grid_ref, row_ref, col_ref, re_ref, im_ref):
    blocks, slots = re_ref.shape
    row = row_ref[...].astype(f32)
    cells = jnp.concatenate([grid_ref[:, :S], grid_ref[:, S:]], axis=0)
    sums = jnp.dot(jnp.concatenate([cells, cells], axis=1), col_ref[...], preferred_element_type=f32)
    for part, out_ref in ((0, re_ref), (1, im_ref)):
        values = jnp.sum(sums[part * S : (part + 1) * S] * row, axis=0, keepdims=True)
        for b in range(blocks):
            out_ref[b : b + 1, :] = values[:, b * slots : (b + 1) * slots]


def degrid(grid, row, col, blocks, slots):
    shape = jax.ShapeDtypeStruct((blocks, slots), f32)
    return pl.pallas_call(
        degrid_kernel,
        in_specs=[VMEM] * 3,
        out_specs=[VMEM] * 2,
        out_shape=[shape] * 2,
        compiler_params=PARAMS,
        name="degrid",
    )(grid, row, col)


def exchange(x, axis):
    return lax.all_to_all(x, axis, split_axis=0, concat_axis=0, tiled=True)


def local(sky_re, sky_im, col_offsets, sub_offsets, kernel, vis_count, cell_index, frac_index):
    pixels = sky_re.shape[1]
    n_sub = sub_offsets.shape[0]
    col = lax.axis_size("col")
    blocks, slots = cell_index.shape[2:]
    band = exchange(first_axis(col_offsets, sky_re[0], sky_im[0]), "col")
    start = (lax.axis_index("facet") * pixels).astype(jnp.int32).reshape(1)
    row, column = weights(vis_count[0], kernel, cell_index[:, 0], frac_index[:, 0])
    band, row, column = lax.optimization_barrier((band, row, column))
    terms = second_axis(band, *second_table(start, sub_offsets, READY))
    arrived = exchange(terms.reshape(n_sub, 8, 2 * S), "facet")
    grid = exchange(own_rows(arrived, col), "col").reshape(S, 2 * S)
    vis_re, vis_im = degrid(grid, row, column, blocks, slots)
    return vis_re[None], vis_im[None]


def solution(mesh):
    placed = (
        P("facet", None, "col"),
        P("facet", None, "col"),
        P(),
        P(),
        P(),
        P("facet", "col"),
        P(None, "facet", "col", None),
        P(None, "facet", "col", None),
    )
    return jax.shard_map(
        local,
        mesh=mesh,
        in_specs=placed,
        out_specs=(P("facet", "col", None), P("facet", "col", None)),
        check_vma=False,
    )
```
